128 devices in a mesh: tm: 32 (over x, z, y_hi), head: 4 (over y_lo, core).
Axes of the slice: x: 4, y: 4 (y_hi: 2, y_lo: 2; y = y_hi * 2 + y_lo), z: 4, core: 2. Of those that a mesh axis runs over, the one named last changes fastest.
Arguments:
- query_raw: bfloat16 [16384, 2560], P('tm', 'head'), may hold values from -100 to 100
- key_raw: bfloat16 [16384, 2560], P('tm', 'head'), may hold values from -100 to 100
- values: bfloat16 [16384, 2560], P('tm', 'head'), may hold values from -6 to 6
- query_gain: float32 [2560], P('head'), may hold values from 0.1 to 1.9
- key_gain: float32 [2560], P('head'), may hold values from 0.1 to 1.9
- out_grad: bfloat16 [16384, 2560], P('tm', 'head'), may hold values from -60 to 60
- block_mask: int32 [128, 20], replicated, may hold values 0 or 1
- band_strides: int32 [3], replicated, may hold values from 1 to 16, as said below
Outputs:
- attended: bfloat16 [16384, 2560], P('tm', 'head')
- query_grad: bfloat16 [16384, 2560], P('tm', 'head')
- key_grad: bfloat16 [16384, 2560], P('tm', 'head')
- value_grad: bfloat16 [16384, 2560], P('tm', 'head')
- query_gain_grad: float32 [2560], P('head')
- key_gain_grad: float32 [2560], P('head')
The draws below stay inside these ranges and needn't reach their ends.
Inputs may be any that keep to these rules, and one draw needn't show every extreme that they name: `band_strides`: entry 0 is 1; every other entry is 2 or more; at least one entry of 1 to 2 is 2 to the power 2 + 2.
All inputs are finite; a program needn't handle non-finite values.
Results may differ from the reference program's by a relative error of at most 0.019.
Values may be sent and summed in bfloat16 or wider, within the bound.
No kernel may reach another device: no remote copies, remote signals or barrier semaphores. Data moves between devices by JAX's collectives and lax.ppermute only.
A program may use at most 128 MiB of HBM per device.

```python
import math
import jax
import jax.numpy as jnp
from jax import lax

HEADS = 20
HEAD_DIM = 128
BLK = 128
WIN = 2
TOK_DEV = 512
TOKENS = 16384
D_ATTN = 2560
BLOCKS = 128
KEY_BLOCKS = 20
N_TM = 32


def shape_field(key, rough_part):
    row_power = jax.random.uniform(jax.random.fold_in(key, 2), (TOKENS, 1), jnp.float32)
    column_power = 0.5 * jnp.arange(D_ATTN, dtype=jnp.float32)[None, :] / (D_ATTN - 1) + 0.5 * jax.random.uniform(jax.random.fold_in(key, 3), (1, D_ATTN), jnp.float32)
    return rough_part * 10.0 ** row_power * 10.0 ** column_power


def draw_query_raw(key, part):
    key = jax.random.fold_in(key, 11)
    rough_part = jax.random.normal(jax.random.fold_in(key, 1), (TOKENS, D_ATTN), jnp.float32)
    field_rows = shape_field(key, rough_part)
    return jnp.clip(field_rows, -100.0, 100.0).astype(jnp.bfloat16)


def draw_key_raw(key, part):
    key = jax.random.fold_in(key, 12)
    rough_part = jax.random.normal(jax.random.fold_in(key, 1), (TOKENS, D_ATTN), jnp.float32)
    field_rows = shape_field(key, rough_part)
    return jnp.clip(field_rows, -100.0, 100.0).astype(jnp.bfloat16)


def draw_out_grad(key, part):
    key = jax.random.fold_in(key, 13)
    position = jnp.arange(TOKENS, dtype=jnp.float32)[:, None] / TOKENS
    rough_part = jax.random.normal(jax.random.fold_in(key, 1), (TOKENS, D_ATTN), jnp.float32)
    row_rise = 3.0 ** position
    return jnp.clip(rough_part * row_rise, -60.0, 60.0).astype(jnp.bfloat16)


def draw_band_strides(key, part):
    key = jax.random.fold_in(key, 17)
    top_stride = 2 ** (WIN + 2)
    level = jnp.arange(WIN + 1, dtype=jnp.int32)
    picked_level = jax.random.randint(jax.random.fold_in(key, 1), (), 1, WIN + 1, dtype=jnp.int32)
    others = jax.random.randint(jax.random.fold_in(key, 2), (WIN + 1,), 2, top_stride + 1, dtype=jnp.int32)
    strides = jnp.where(level == picked_level, jnp.int32(top_stride), others)
    return jnp.where(level == 0, jnp.int32(1), strides).astype(jnp.int32)


def touch_ends(array, rng, least, largest):
    extent = array.shape
    index_at = [jax.random.randint(jax.random.fold_in(rng, axis), (), 0, extent[axis]) for axis in range(len(extent))]
    array = array.at[tuple(index_at)].set(least)
    longest = extent.index(max(extent))
    index_at[longest] = (index_at[longest] + 1) % extent[longest]
    return array.at[tuple(index_at)].set(largest)


def steps_of(own_key, extent, shards, least, high):
    loudness, own = 1.0, jax.random.fold_in(own_key, 6)
    for dim, blocks in shards:
        heights = jnp.exp(jax.random.uniform(jax.random.fold_in(own, dim), (blocks,), jnp.float32, least / len(shards), high / len(shards)))
        loudness = loudness * jnp.repeat(heights, extent[dim] // blocks).reshape([-1 if axis == dim else 1 for axis in range(len(extent))])
    return loudness


def scatter_about(rng, dims, width, bound, shards=(), held_as=jnp.bfloat16):
    values = jax.random.normal(rng, dims, jnp.float32) * width
    if len(shards) > 0:
        values = steps_of(rng, dims, shards, -0.22, 0.18) * values
    return jnp.clip(values, min=-bound, max=bound).astype(held_as)


def setup_inputs(seed: int = 0) -> dict:
    keys = jax.random.split(jax.random.key(seed), 9)
    return {
        "query_raw": draw_query_raw(jax.random.fold_in(keys[8], 71), 0),
        "key_raw": draw_key_raw(jax.random.fold_in(keys[8], 71), 0),
        "values": scatter_about(keys[2], (TOKENS, D_ATTN), 1.0, 6.0, ((0, 32), (1, 4))),
        "query_gain": jnp.clip(1.0 + 0.18 * jax.random.normal(keys[3], (D_ATTN,), jnp.float32), 0.1, 1.9),
        "key_gain": jnp.clip(1.0 + 0.18 * jax.random.normal(keys[4], (D_ATTN,), jnp.float32), 0.1, 1.9),
        "out_grad": draw_out_grad(jax.random.fold_in(keys[8], 71), 0),
        "block_mask": touch_ends((jax.random.randint(keys[6], (BLOCKS, KEY_BLOCKS), 0, 4) < 3).astype(jnp.int32), jax.random.fold_in(keys[6], 1), 0, 1),
        "band_strides": draw_band_strides(jax.random.fold_in(keys[8], 71), 0),
    }


NORM_EPSILON = 1e-06

def live_blocks(chain_pos, mask_rows, band_strides, groups):
    blocks_here = mask_rows.shape[0]
    column = jnp.arange(mask_rows.shape[1], dtype=jnp.int32)
    offset = column // blocks_here - WIN
    key_group = chain_pos + offset
    query_block = chain_pos * blocks_here + jnp.arange(blocks_here, dtype=jnp.int32)
    key_block = key_group * blocks_here + column % blocks_here
    separation = jnp.abs(offset)
    levels = jnp.arange(WIN + 1, dtype=jnp.int32)
    stride = lax.optimization_barrier(jnp.sum(jnp.where(separation[:, None] == levels[None, :], band_strides[None, :], 0), axis=1))
    inside = (key_group >= 0) & (key_group < groups)
    stride_hit = (query_block[:, None] + key_block[None, :]) % stride[None, :] == 0
    aligned = (query_block % blocks_here)[:, None] == (key_block % blocks_here)[None, :]
    return ((mask_rows == 1) & stride_hit | aligned) & inside[None, :]

def expand(live_pairs):
    return jnp.repeat(jnp.repeat(live_pairs, BLK, axis=0), BLK, axis=1)

def normalize(raw_rows, gain_vector):
    raw_float = raw_rows.astype(jnp.float32)
    inverse = lax.rsqrt(lax.optimization_barrier(jnp.mean(raw_float * raw_float, axis=1, keepdims=True)) + NORM_EPSILON)
    unit_rows = raw_float * inverse
    return (unit_rows, inverse, (unit_rows * gain_vector[None, :]).astype(jnp.bfloat16))

def restore(grad_normed, unit_rows, inverse, gain_vector):
    scaled = grad_normed * gain_vector[None, :]
    inner = lax.optimization_barrier(jnp.mean(scaled * unit_rows, axis=1, keepdims=True))
    return ((inverse * (scaled - unit_rows * inner)).astype(jnp.bfloat16), lax.optimization_barrier(jnp.sum(grad_normed * unit_rows, axis=0)))

def rounded(matrix):
    return lax.optimization_barrier(matrix.astype(jnp.bfloat16)).astype(jnp.float32)

def reference(query_raw, key_raw, values, query_gain, key_gain, out_grad, block_mask, band_strides):
    groups = N_TM
    tok_rows = TOK_DEV
    features = D_ATTN
    window_rows = (2 * WIN + 1) * tok_rows
    blocks_here = tok_rows // BLK
    score_scale = 1.0 / math.sqrt(HEAD_DIM)
    query_unit, query_inverse, query_normed = normalize(query_raw, query_gain)
    key_unit, key_inverse, key_normed = normalize(key_raw, key_gain)
    margin = WIN * tok_rows
    key_padded = jnp.pad(key_normed, ((margin, margin), (0, 0)))
    value_padded = jnp.pad(values, ((margin, margin), (0, 0)))

    def pieces(chain_pos):
        first_row = chain_pos * tok_rows
        query_group = lax.dynamic_slice_in_dim(query_normed, first_row, tok_rows, 0).astype(jnp.float32).reshape(tok_rows, HEADS, HEAD_DIM)
        key_group = lax.dynamic_slice_in_dim(key_padded, first_row, window_rows, 0).astype(jnp.float32).reshape(window_rows, HEADS, HEAD_DIM)
        value_group = lax.dynamic_slice_in_dim(value_padded, first_row, window_rows, 0).astype(jnp.float32).reshape(window_rows, HEADS, HEAD_DIM)
        mask_rows = lax.dynamic_slice_in_dim(block_mask, chain_pos * blocks_here, blocks_here, 0)
        live_pairs = expand(live_blocks(chain_pos, mask_rows, band_strides, groups))
        scores = jnp.einsum('qhe,khe->hqk', query_group, key_group) * score_scale
        return (query_group, key_group, value_group, live_pairs, scores)

    def forward(chain_pos):
        query_group, key_group, value_group, live_pairs, scores = pieces(chain_pos)
        masked = jnp.where(live_pairs[None], scores, -jnp.inf)
        row_top = lax.optimization_barrier(jnp.max(masked, axis=2))
        weights = jnp.exp(masked - row_top[:, :, None])
        row_total = lax.optimization_barrier(jnp.sum(weights, axis=2))
        head_out = jnp.einsum('hqk,khe->qhe', rounded(weights), value_group) / jnp.transpose(row_total)[:, :, None]
        return (head_out.reshape(tok_rows, features).astype(jnp.bfloat16), row_top + jnp.log(row_total))
    attended, lse_rows = lax.map(forward, jnp.arange(groups, dtype=jnp.int32))
    attended = attended.reshape(groups * tok_rows, features)
    products = attended.astype(jnp.float32) * out_grad.astype(jnp.float32)
    row_dots = lax.optimization_barrier(jnp.sum(products.reshape(groups, tok_rows, HEADS, HEAD_DIM), axis=3))

    def backward(accumulated, chain_pos):
        key_accum, value_accum = accumulated
        query_group, key_group, value_group, live_pairs, scores = pieces(chain_pos)
        attn_probs = jnp.where(live_pairs[None], jnp.exp(scores - lse_rows[chain_pos][:, :, None]), 0.0)
        grad_group = lax.dynamic_slice_in_dim(out_grad, chain_pos * tok_rows, tok_rows, 0).astype(jnp.float32).reshape(tok_rows, HEADS, HEAD_DIM)
        grad_probs = jnp.einsum('qhe,khe->hqk', grad_group, value_group)
        score_grad = rounded(attn_probs * (grad_probs - jnp.transpose(row_dots[chain_pos])[:, :, None]))
        query_part = jnp.einsum('hqk,khe->qhe', score_grad, key_group) * score_scale
        key_part = jnp.einsum('hqk,qhe->khe', score_grad, query_group) * score_scale
        value_part = jnp.einsum('hqk,qhe->khe', rounded(attn_probs), grad_group)
        first_row = chain_pos * tok_rows
        key_accum = lax.dynamic_update_slice_in_dim(key_accum, lax.dynamic_slice_in_dim(key_accum, first_row, window_rows, 0) + key_part.reshape(window_rows, features), first_row, 0)
        value_accum = lax.dynamic_update_slice_in_dim(value_accum, lax.dynamic_slice_in_dim(value_accum, first_row, window_rows, 0) + value_part.reshape(window_rows, features), first_row, 0)
        return ((key_accum, value_accum), query_part.reshape(tok_rows, features))
    zero_rows = jnp.zeros((groups * tok_rows + 2 * margin, features), jnp.float32)
    (key_accum, value_accum), query_parts = lax.scan(backward, (zero_rows, zero_rows), jnp.arange(groups, dtype=jnp.int32))
    grad_query = query_parts.reshape(groups * tok_rows, features)
    grad_key = key_accum[margin:margin + groups * tok_rows]
    value_grad = value_accum[margin:margin + groups * tok_rows].astype(jnp.bfloat16)
    query_grad, query_gain_grad = restore(grad_query, query_unit, query_inverse, query_gain)
    key_grad, key_gain_grad = restore(grad_key, key_unit, key_inverse, key_gain)
    return (attended, query_grad, key_grad, value_grad, query_gain_grad, key_gain_grad)
```

```python
import functools
import math

import jax
import jax.numpy as jnp
from jax import lax
from jax.experimental import pallas as pl
from jax.experimental.pallas import tpu as pltpu
from jax.sharding import PartitionSpec as P

HEAD_DIM = 128
BLK = 128
WIN = 2
BLOCKS_HERE = 4
TOK = BLK * BLOCKS_HERE
WINDOWS = 6
ROUNDS = 12
NORM_EPSILON = 1e-06
DEAD = -1e30
SCALE = 1.0 / math.sqrt(HEAD_DIM)
LOG2E = math.log2(math.e)
LN2 = math.log(2.0)


def shifted(value, axis, steps):
    count = lax.axis_size(axis)
    pairs = [(s, s + steps) for s in range(count) if 0 <= s + steps < count]
    return lax.ppermute(value, axis, pairs)


def swapped(value, axis):
    return lax.ppermute(value, axis, [(s, s ^ 1) for s in range(lax.axis_size(axis))])


def contract(left, right, left_dim, right_dim):
    return lax.dot_general(
        left, right, (((left_dim,), (right_dim,)), ((), ())), preferred_element_type=jnp.float32
    )


def live_tables(chain_pos, groups, block_mask, band_strides):
    partner = chain_pos ^ 1
    query_groups = jnp.stack([chain_pos, partner])
    window_groups = jnp.stack(
        [chain_pos, partner, chain_pos - 2, partner - 2, chain_pos + 2, partner + 2]
    )
    apart = window_groups[None, :] - query_groups[:, None]
    inside = (window_groups >= 0) & (window_groups < groups)
    near = (jnp.abs(apart) <= WIN) & inside[None, :]
    pair_first = (chain_pos // 2) * 2 * BLOCKS_HERE
    pair_mask = lax.dynamic_slice_in_dim(block_mask, pair_first, 2 * BLOCKS_HERE, 0)
    pair_mask = pair_mask.reshape(2, BLOCKS_HERE, 2 * WIN + 1, BLOCKS_HERE)
    masks = jnp.where(chain_pos % 2 == 0, pair_mask, pair_mask[::-1])
    levels = jnp.arange(2 * WIN + 1, dtype=jnp.int32) - WIN
    picked = jnp.sum(
        jnp.where(
            apart[:, None, :, None, None] == levels[None, None, None, :, None],
            masks[:, :, None, :, :],
            0,
        ),
        axis=3,
    )
    stride = jnp.sum(
        jnp.where(
            jnp.abs(apart)[:, :, None] == jnp.arange(WIN + 1, dtype=jnp.int32),
            band_strides,
            0,
        ),
        axis=2,
    )
    stride = jnp.maximum(stride, 1)
    within = jnp.arange(BLOCKS_HERE, dtype=jnp.int32)
    query_block = query_groups[:, None] * BLOCKS_HERE + within[None, :]
    key_block = window_groups[:, None] * BLOCKS_HERE + within[None, :]
    total = query_block[:, :, None, None] + key_block[None, None, :, :]
    hit = total % stride[:, None, :, None] == 0
    aligned = within[:, None] == within[None, :]
    live = ((picked == 1) & hit | aligned[None, :, None, :]) & near[:, None, :, None]
    centre = jnp.stack([live[0, :, 0, :], live[1, :, 1, :]])
    slots = jnp.arange(WINDOWS, dtype=jnp.int32)
    is_centre = slots[None, :] == jnp.arange(2, dtype=jnp.int32)[:, None]
    scattered = live & ~aligned[None, :, None, :] & ~is_centre[:, None, :, None]
    scattered = scattered.reshape(2, BLOCKS_HERE, WINDOWS * BLOCKS_HERE)
    rank = jnp.cumsum(scattered.astype(jnp.int32), axis=2) - 1
    rounds = jnp.arange(ROUNDS, dtype=jnp.int32)
    chosen = scattered[:, None] & (rank[:, None] == rounds[None, :, None, None])
    places = jnp.arange(WINDOWS * BLOCKS_HERE, dtype=jnp.int32)
    place = jnp.sum(jnp.where(chosen, places, 0), axis=3)
    used = jnp.any(chosen, axis=3)
    count = jnp.max(jnp.sum(scattered.astype(jnp.int32), axis=2), axis=1)
    side = chain_pos % 2
    offs = jnp.stack(
        [
            jnp.stack([jnp.int32(1), jnp.int32(2), jnp.int32(4), 3 + 2 * side]),
            jnp.stack([jnp.int32(0), jnp.int32(3), jnp.int32(5), 4 - 2 * side]),
        ]
    )
    off_inside = jnp.sum(
        jnp.where(offs[:, :, None] == slots[None, None, :], near[:, None, :].astype(jnp.int32), 0),
        axis=2,
    )
    ints = jnp.concatenate([place.reshape(2, -1), offs, count[:, None]], axis=1)
    flags = jnp.concatenate(
        [used.reshape(2, -1), centre.reshape(2, -1), off_inside == 1], axis=1
    )
    return ints, jnp.where(flags, 0.0, DEAD).astype(jnp.float32)


INT_OFFS = ROUNDS * BLOCKS_HERE
INT_COUNT = INT_OFFS + 4
BIAS_CENTRE = ROUNDS * BLOCKS_HERE
BIAS_OFF = BIAS_CENTRE + 16


def fold_rows(tile, op):
    return op(tile.reshape(BLK // 8, 8, BLK), axis=0)


def attention_kernel(
    groups_here,
    ints,
    bias,
    query,
    grad,
    own,
    partner,
    before_own,
    before_partner,
    after_own,
    after_partner,
    key_inverse,
    key_gain,
    attended,
    grad_query,
    to_before,
    to_after,
    local,
    keys,
    keys_t,
    vals,
    vals_t,
    off_keys,
    off_vals,
    off_keys_t,
    off_vals_t,
    grad_keys,
    grad_vals,
    centre_w,
    centre_b,
    centre_d,
    off_w,
    off_b,
    off_d,
    extra_w,
    extra_b,
    out_t,
    top_rows,
    sum_rows,
    grad_scaled,
):
    gain = key_gain[...]
    windows = (own, partner, before_own, before_partner, after_own, after_partner)
    for w, ref in enumerate(windows):
        for j in range(BLOCKS_HERE):
            rows = pl.ds(j * BLK, BLK)
            normed = (ref[0, rows, :].astype(jnp.float32) * key_inverse[w, rows, :] * gain).astype(
                jnp.bfloat16
            )
            value = ref[1, rows, :]
            keys[w * 4 + j] = normed
            vals[w * 4 + j] = value
            keys_t[w * 4 + j] = normed.T
            vals_t[w * 4 + j] = value.T
    grad_keys[...] = jnp.zeros_like(grad_keys)
    grad_vals[...] = jnp.zeros_like(grad_vals)

    def group_task(g, carry):
        centre = g * 4
        rounds = ints[g, INT_COUNT]
        offs = [ints[g, INT_OFFS + o] * 4 for o in range(4)]

        def rows_of(i):
            return pl.ds(i * BLK, BLK)

        def gather_off(o, c):
            at = ints[g, INT_OFFS + o] * 4
            there = pl.ds(pl.multiple_of(o * BLK, BLK), BLK)
            for i in range(4):
                off_keys[i, there, :] = keys[at + i]
                off_vals[i, there, :] = vals[at + i]
                off_keys_t[i, :, there] = keys_t[at + i]
                off_vals_t[i, :, there] = vals_t[at + i]
            return c

        lax.fori_loop(0, 4, gather_off, 0)

        query_all = query[g]
        query_rows = [query[g, rows_of(i), :] for i in range(4)]
        centre_keys = keys[pl.ds(centre, 4)].reshape(TOK, HEAD_DIM)
        for i in range(4):
            off_w[i] = contract(off_keys[i], query_rows[i], 1, 1)
        centre_w[...] = contract(centre_keys, query_all, 1, 1)
        for i in range(4):
            best = None
            for j in range(4):
                part = fold_rows(centre_w[rows_of(j), rows_of(i)], jnp.max)
                part = part + bias[g, BIAS_CENTRE + i * 4 + j]
                best = part if best is None else jnp.maximum(best, part)
            for o in range(4):
                part = fold_rows(off_w[i, rows_of(o), :], jnp.max) + bias[g, BIAS_OFF + o]
                best = jnp.maximum(best, part)
            top_rows[i] = best

        def extra_scores(r, c):
            for i in range(4):
                scores = contract(keys[ints[g, r * 4 + i]], query_rows[i], 1, 1)
                extra_w[r * 4 + i] = scores
                part = fold_rows(scores, jnp.max) + bias[g, r * 4 + i]
                top_rows[i] = jnp.maximum(top_rows[i], part)
            return c

        lax.fori_loop(0, rounds, extra_scores, 0)
        tops = [jnp.max(top_rows[i], axis=0, keepdims=True) for i in range(4)]

        for i in range(4):
            total = None
            for j in range(4):
                less = tops[i] - bias[g, BIAS_CENTRE + i * 4 + j]
                weight = jnp.exp2(centre_w[rows_of(j), rows_of(i)] - less)
                centre_w[rows_of(j), rows_of(i)] = weight
                centre_b[rows_of(j), rows_of(i)] = weight.astype(jnp.bfloat16)
                part = fold_rows(weight, jnp.sum)
                total = part if total is None else total + part
            for o in range(4):
                less = tops[i] - bias[g, BIAS_OFF + o]
                weight = jnp.exp2(off_w[i, rows_of(o), :] - less)
                off_w[i, rows_of(o), :] = weight
                off_b[i, rows_of(o), :] = weight.astype(jnp.bfloat16)
                total = total + fold_rows(weight, jnp.sum)
            sum_rows[i] = total
        centre_vals_t = jnp.concatenate([vals_t[centre + j] for j in range(4)], axis=1)
        centre_out = contract(centre_vals_t, centre_b[...], 1, 0)
        for i in range(4):
            out_t[i] = centre_out[:, i * BLK : (i + 1) * BLK] + contract(
                off_vals_t[i], off_b[i], 1, 0
            )

        def extra_out(r, c):
            for i in range(4):
                less = tops[i] - bias[g, r * 4 + i]
                weight = jnp.exp2(extra_w[r * 4 + i] - less)
                extra_w[r * 4 + i] = weight
                weight_b = weight.astype(jnp.bfloat16)
                extra_b[r * 4 + i] = weight_b
                sum_rows[i] = sum_rows[i] + fold_rows(weight, jnp.sum)
                out_t[i] = out_t[i] + contract(vals_t[ints[g, r * 4 + i]], weight_b, 1, 0)
            return c

        lax.fori_loop(0, rounds, extra_out, 0)

        dots = []
        for i in range(4):
            inverse = 1.0 / jnp.sum(sum_rows[i], axis=0, keepdims=True)
            head_out = (out_t[i] * inverse).astype(jnp.bfloat16)
            attended[g, rows_of(i), :] = head_out.T
            grad_t = grad[g, rows_of(i), :].T.astype(jnp.float32) * inverse
            dots.append(jnp.sum(grad_t * head_out.astype(jnp.float32), axis=0, keepdims=True))
            grad_scaled[rows_of(i), :] = grad_t.astype(jnp.bfloat16).T

        grad_rows = [grad_scaled[rows_of(i), :] for i in range(4)]
        centre_vals = vals[pl.ds(centre, 4)].reshape(TOK, HEAD_DIM)
        flow = contract(centre_vals, grad_scaled[...], 1, 1)
        for i in range(4):
            for j in range(4):
                piece = flow[j * BLK : (j + 1) * BLK, i * BLK : (i + 1) * BLK]
                centre_d[rows_of(j), rows_of(i)] = (
                    centre_w[rows_of(j), rows_of(i)] * (piece - dots[i])
                ).astype(jnp.bfloat16)
            off_flow = contract(off_vals[i], grad_rows[i], 1, 1)
            for o in range(4):
                piece = off_flow[o * BLK : (o + 1) * BLK]
                off_d[i, rows_of(o), :] = (off_w[i, rows_of(o), :] * (piece - dots[i])).astype(
                    jnp.bfloat16
                )
        centre_keys_t = jnp.concatenate([keys_t[centre + j] for j in range(4)], axis=1)
        centre_grad = contract(centre_keys_t, centre_d[...], 1, 0)
        for i in range(4):
            out_t[i] = centre_grad[:, i * BLK : (i + 1) * BLK] + contract(
                off_keys_t[i], off_d[i], 1, 0
            )
        place = pl.ds(centre, 4)
        grad_keys[place] = grad_keys[place] + contract(centre_d[...], query_all, 1, 0).reshape(
            4, BLK, HEAD_DIM
        )
        grad_vals[place] = grad_vals[place] + contract(
            centre_b[...], grad_scaled[...], 1, 0
        ).reshape(4, BLK, HEAD_DIM)
        for i in range(4):
            to_keys = contract(off_d[i], query_rows[i], 1, 0)
            to_vals = contract(off_b[i], grad_rows[i], 1, 0)
            for o in range(4):
                at = offs[o] + i
                grad_keys[at] = grad_keys[at] + to_keys[o * BLK : (o + 1) * BLK]
                grad_vals[at] = grad_vals[at] + to_vals[o * BLK : (o + 1) * BLK]

        def extra_grads(r, c):
            for i in range(4):
                at = ints[g, r * 4 + i]
                piece = contract(vals[at], grad_rows[i], 1, 1)
                score_grad = (extra_w[r * 4 + i] * (piece - dots[i])).astype(jnp.bfloat16)
                out_t[i] = out_t[i] + contract(keys_t[at], score_grad, 1, 0)
                grad_keys[at] = grad_keys[at] + contract(score_grad, query_rows[i], 1, 0)
                grad_vals[at] = grad_vals[at] + contract(extra_b[r * 4 + i], grad_rows[i], 1, 0)
            return c

        lax.fori_loop(0, rounds, extra_grads, 0)
        for i in range(4):
            grad_query[g, rows_of(i), :] = (out_t[i] * SCALE).astype(jnp.bfloat16).T
        return carry

    lax.fori_loop(0, groups_here, group_task, 0)
    for n, (window, source, factor) in enumerate(
        ((0, grad_keys, LN2), (1, grad_keys, LN2), (0, grad_vals, 1.0), (1, grad_vals, 1.0))
    ):
        for j in range(BLOCKS_HERE):
            rows = pl.ds(j * BLK, BLK)
            local[n, rows, :] = source[window * 4 + j] * factor
            to_before[n, rows, :] = (source[(window + 2) * 4 + j] * factor).astype(jnp.bfloat16)
            to_after[n, rows, :] = (source[(window + 4) * 4 + j] * factor).astype(jnp.bfloat16)


def attention_slot(slot, groups_here, ints, bias, query, grad, windows, key_inverse, key_gain):
    token_block = pl.BlockSpec((groups_here, TOK, HEAD_DIM), lambda n: (0, 0, slot))
    window_block = pl.BlockSpec((2, TOK, HEAD_DIM), lambda n: (0, 0, slot))
    table = pl.BlockSpec(memory_space=pltpu.SMEM)
    out_token = pl.BlockSpec((groups_here, TOK, HEAD_DIM), lambda n: (0, 0, 0))
    out_grads = pl.BlockSpec((4, TOK, HEAD_DIM), lambda n: (0, 0, 0))
    tiles = WINDOWS * BLOCKS_HERE
    tile = (BLK, BLK)
    return pl.pallas_call(
        functools.partial(attention_kernel, groups_here),
        grid=(1,),
        in_specs=[table, table, token_block, token_block]
        + [window_block] * WINDOWS
        + [
            pl.BlockSpec((WINDOWS, TOK, 1), lambda n: (0, 0, 0)),
            pl.BlockSpec((1, HEAD_DIM), lambda n: (0, slot)),
        ],
        out_specs=[out_token, out_token, out_grads, out_grads, out_grads],
        out_shape=[
            jax.ShapeDtypeStruct((groups_here, TOK, HEAD_DIM), jnp.bfloat16),
            jax.ShapeDtypeStruct((groups_here, TOK, HEAD_DIM), jnp.bfloat16),
            jax.ShapeDtypeStruct((4, TOK, HEAD_DIM), jnp.bfloat16),
            jax.ShapeDtypeStruct((4, TOK, HEAD_DIM), jnp.bfloat16),
            jax.ShapeDtypeStruct((4, TOK, HEAD_DIM), jnp.float32),
        ],
        scratch_shapes=[
            pltpu.VMEM((tiles,) + tile, jnp.bfloat16),
            pltpu.VMEM((tiles,) + tile, jnp.bfloat16),
            pltpu.VMEM((tiles,) + tile, jnp.bfloat16),
            pltpu.VMEM((tiles,) + tile, jnp.bfloat16),
            pltpu.VMEM((4, TOK, BLK), jnp.bfloat16),
            pltpu.VMEM((4, TOK, BLK), jnp.bfloat16),
            pltpu.VMEM((4, BLK, TOK), jnp.bfloat16),
            pltpu.VMEM((4, BLK, TOK), jnp.bfloat16),
            pltpu.VMEM((tiles,) + tile, jnp.float32),
            pltpu.VMEM((tiles,) + tile, jnp.float32),
            pltpu.VMEM((TOK, TOK), jnp.float32),
            pltpu.VMEM((TOK, TOK), jnp.bfloat16),
            pltpu.VMEM((TOK, TOK), jnp.bfloat16),
            pltpu.VMEM((4, TOK, BLK), jnp.float32),
            pltpu.VMEM((4, TOK, BLK), jnp.bfloat16),
            pltpu.VMEM((4, TOK, BLK), jnp.bfloat16),
            pltpu.VMEM((ROUNDS * 4,) + tile, jnp.float32),
            pltpu.VMEM((ROUNDS * 4,) + tile, jnp.bfloat16),
            pltpu.VMEM((4,) + tile, jnp.float32),
            pltpu.VMEM((4, 8, BLK), jnp.float32),
            pltpu.VMEM((4, 8, BLK), jnp.float32),
            pltpu.VMEM((TOK, HEAD_DIM), jnp.bfloat16),
        ],
        compiler_params=pltpu.CompilerParams(vmem_limit_bytes=40 * 1024 * 1024),
        cost_estimate=pl.CostEstimate(
            flops=groups_here * 40 * 6 * 2 * BLK**3 * 4,
            bytes_accessed=6 * 1024 * 1024,
            transcendentals=groups_here * 40 * BLK * BLK,
        ),
        name="attention_slot",
    )(ints, bias, query, grad, *windows, key_inverse, key_gain)


def shards(query_raw, key_raw, values, query_gain, key_gain, out_grad, block_mask, band_strides):
    features = query_raw.shape[1]
    groups = lax.axis_size("tm")
    chain_pos = lax.axis_index("tm")
    even = chain_pos % 2 == 0
    all_features = features * lax.axis_size("head")
    half = 2 * HEAD_DIM

    def keep(x):
        return jnp.where(even, x[..., :half], x[..., half : 2 * half])

    def give(x):
        return jnp.where(even, x[..., half : 2 * half], x[..., :half])

    def last(x):
        return x[..., 2 * half :]

    key_values = jnp.stack([key_raw, values])
    own_keys = jnp.concatenate([keep(key_values), last(key_values)], axis=2)
    pair_keys = jnp.concatenate([give(key_values), last(key_values)], axis=2)
    partner_keys = swapped(pair_keys, "tm")
    before_own = shifted(own_keys, "tm", 2)
    after_own = shifted(own_keys, "tm", -2)
    before_partner = shifted(partner_keys, "tm", 2)
    after_partner = shifted(partner_keys, "tm", -2)
    windows = (own_keys, partner_keys, before_own, before_partner, after_own, after_partner)

    query_float = query_raw.astype(jnp.float32)
    key_float = key_raw.astype(jnp.float32)
    squares = lax.psum(
        jnp.stack([jnp.sum(query_float * query_float, axis=1), jnp.sum(key_float * key_float, axis=1)]),
        "head",
    )
    inverses = lax.rsqrt(squares / all_features + NORM_EPSILON)
    query_inverse = inverses[0][:, None]
    key_inverse = inverses[1][:, None]
    pair_inverse = jnp.stack([inverses[1], swapped(inverses[1], "tm")])
    all_inverses = jnp.concatenate(
        [pair_inverse, shifted(pair_inverse, "tm", 2), shifted(pair_inverse, "tm", -2)]
    )[:, :, None]

    query_unit = query_float * query_inverse
    key_unit = key_float * key_inverse
    query_scaled = (query_unit * (query_gain * (SCALE * LOG2E))[None, :]).astype(jnp.bfloat16)
    given = swapped(jnp.stack([give(query_scaled), give(out_grad)]), "tm")
    query_pair = jnp.stack([keep(query_scaled), given[0]])
    grad_pair = jnp.stack([keep(out_grad), given[1]])
    ints, bias = live_tables(chain_pos, groups, block_mask, band_strides)
    slot_gain = jnp.concatenate([keep(key_gain), last(key_gain)])[None, :]

    results = []
    for slot in range(3):
        if slot < 2:
            args = (query_pair, grad_pair)
            res = attention_slot(slot, 2, ints, bias, *args, windows, all_inverses, slot_gain)
        else:
            spec_query = jnp.concatenate([keep(query_scaled), last(query_scaled)], axis=1)[None]
            spec_grad = jnp.concatenate([keep(out_grad), last(out_grad)], axis=1)[None]
            res = attention_slot(
                slot, 1, ints, bias, spec_query, spec_grad, windows, all_inverses, slot_gain
            )
        results.append(res)

    given_grads = []
    kept_grads = []
    for attended_part, query_part, to_before, to_after, local in results:
        total = (
            local
            + shifted(to_before, "tm", -2).astype(jnp.float32)
            + shifted(to_after, "tm", 2).astype(jnp.float32)
        )
        kept_grads.append(jnp.stack([total[0], total[2]]))
        given_grads.append(
            swapped(jnp.stack([total[1], total[3]]).astype(jnp.bfloat16), "tm").astype(jnp.float32)
        )
    outs = swapped(
        jnp.stack(
            [
                jnp.concatenate([results[0][0][1], results[1][0][1]], axis=1),
                jnp.concatenate([results[0][1][1], results[1][1][1]], axis=1),
            ]
        ),
        "tm",
    )

    def placed(mine, theirs, rest):
        first = jnp.where(even, mine, theirs)
        second = jnp.where(even, theirs, mine)
        return jnp.concatenate([first, second, rest], axis=-1)

    attended = placed(
        jnp.concatenate([results[0][0][0], results[1][0][0]], axis=1), outs[0], results[2][0][0]
    )
    grad_query = placed(
        jnp.concatenate([results[0][1][0], results[1][1][0]], axis=1), outs[1], results[2][1][0]
    ).astype(jnp.float32)
    grads = placed(
        jnp.concatenate([kept_grads[0], kept_grads[1]], axis=2),
        jnp.concatenate([given_grads[0], given_grads[1]], axis=2),
        kept_grads[2] + given_grads[2],
    )
    grad_key = grads[0]
    grad_value = grads[1].astype(jnp.bfloat16)
    query_back = grad_query * query_gain[None, :]
    key_back = grad_key * key_gain[None, :]
    inner = lax.psum(
        jnp.stack([jnp.sum(query_back * query_unit, axis=1), jnp.sum(key_back * key_unit, axis=1)]),
        "head",
    )
    inner = inner / all_features
    query_grad = (query_inverse * (query_back - query_unit * inner[0][:, None])).astype(jnp.bfloat16)
    key_grad = (key_inverse * (key_back - key_unit * inner[1][:, None])).astype(jnp.bfloat16)
    gains = jnp.stack([jnp.sum(grad_query * query_unit, axis=0), jnp.sum(grad_key * key_unit, axis=0)])
    step = 1
    while step < groups:
        gains = gains + lax.ppermute(gains, "tm", [(s, s ^ step) for s in range(groups)])
        step *= 2
    return (attended, query_grad, key_grad, grad_value, gains[0], gains[1])


def solution(mesh):
    placed = (
        P("tm", "head"),
        P("tm", "head"),
        P("tm", "head"),
        P("head"),
        P("head"),
        P("tm", "head"),
        P(),
        P(),
    )
    return jax.shard_map(
        shards,
        mesh=mesh,
        in_specs=placed,
        out_specs=(
            P("tm", "head"),
            P("tm", "head"),
            P("tm", "head"),
            P("tm", "head"),
            P("head"),
            P("head"),
        ),
        check_vma=False,
    )
```

```python
import functools
import math

import jax
import jax.numpy as jnp
from jax import lax
from jax.experimental import pallas as pl
from jax.experimental.pallas import tpu as pltpu
from jax.sharding import PartitionSpec as P

HEAD_DIM = 128
BLK = 128
WIN = 2
BLOCKS_HERE = 4
TOK = BLK * BLOCKS_HERE
WINDOWS = 6
ROUNDS = 12
NORM_EPSILON = 1e-06
DEAD = -1e30
SCALE = 1.0 / math.sqrt(HEAD_DIM)
LOG2E = math.log2(math.e)
LN2 = math.log(2.0)


def to_near(value, axis):
    return lax.ppermute(value, axis, [(s, s ^ 2) for s in range(lax.axis_size(axis))])


def to_far(value, axis):
    count = lax.axis_size(axis)
    pairs = [(s, s - 2 if s // 2 % 2 == 0 else s + 2) for s in range(count)]
    return lax.ppermute(value, axis, [(s, d) for s, d in pairs if 0 <= d < count])


def swapped(value, axis):
    return lax.ppermute(value, axis, [(s, s ^ 1) for s in range(lax.axis_size(axis))])


def summed_over_groups(value):
    count = lax.axis_size("tm")
    unit = 1
    while unit < count:
        radix = 4 if unit > 1 else 2
        parts = []
        for turn in range(1, radix):
            pairs = []
            for s in range(count):
                digit = s // unit % radix
                pairs.append((s, s + ((digit + turn) % radix - digit) * unit))
            parts.append(lax.ppermute(value, "tm", pairs))
        for part in parts:
            value = value + part
        unit *= radix
    return value


def contract(left, right, left_dim, right_dim):
    return lax.dot_general(
        left, right, (((left_dim,), (right_dim,)), ((), ())), preferred_element_type=jnp.float32
    )


def live_tables(chain_pos, groups, block_mask, band_strides):
    partner = chain_pos ^ 1
    query_groups = jnp.stack([chain_pos, partner])
    near_step = jnp.where(chain_pos // 2 % 2 == 0, 2, -2)
    window_groups = jnp.stack(
        [
            chain_pos,
            partner,
            chain_pos + near_step,
            partner + near_step,
            chain_pos - near_step,
            partner - near_step,
        ]
    )
    apart = window_groups[None, :] - query_groups[:, None]
    inside = (window_groups >= 0) & (window_groups < groups)
    near = (jnp.abs(apart) <= WIN) & inside[None, :]
    pair_first = (chain_pos // 2) * 2 * BLOCKS_HERE
    pair_mask = lax.dynamic_slice_in_dim(block_mask, pair_first, 2 * BLOCKS_HERE, 0)
    pair_mask = pair_mask.reshape(2, BLOCKS_HERE, 2 * WIN + 1, BLOCKS_HERE)
    masks = jnp.where(chain_pos % 2 == 0, pair_mask, pair_mask[::-1])
    levels = jnp.arange(2 * WIN + 1, dtype=jnp.int32) - WIN
    picked = jnp.sum(
        jnp.where(
            apart[:, None, :, None, None] == levels[None, None, None, :, None],
            masks[:, :, None, :, :],
            0,
        ),
        axis=3,
    )
    stride = jnp.sum(
        jnp.where(
            jnp.abs(apart)[:, :, None] == jnp.arange(WIN + 1, dtype=jnp.int32),
            band_strides,
            0,
        ),
        axis=2,
    )
    stride = jnp.maximum(stride, 1)
    within = jnp.arange(BLOCKS_HERE, dtype=jnp.int32)
    query_block = query_groups[:, None] * BLOCKS_HERE + within[None, :]
    key_block = window_groups[:, None] * BLOCKS_HERE + within[None, :]
    total = query_block[:, :, None, None] + key_block[None, None, :, :]
    hit = total % stride[:, None, :, None] == 0
    aligned = within[:, None] == within[None, :]
    live = ((picked == 1) & hit | aligned[None, :, None, :]) & near[:, None, :, None]
    centre = jnp.stack([live[0, :, 0, :], live[1, :, 1, :]])
    slots = jnp.arange(WINDOWS, dtype=jnp.int32)
    is_centre = slots[None, :] == jnp.arange(2, dtype=jnp.int32)[:, None]
    scattered = live & ~aligned[None, :, None, :] & ~is_centre[:, None, :, None]
    scattered = scattered.reshape(2, BLOCKS_HERE, WINDOWS * BLOCKS_HERE)
    rank = jnp.cumsum(scattered.astype(jnp.int32), axis=2) - 1
    rounds = jnp.arange(ROUNDS, dtype=jnp.int32)
    chosen = scattered[:, None] & (rank[:, None] == rounds[None, :, None, None])
    places = jnp.arange(WINDOWS * BLOCKS_HERE, dtype=jnp.int32)
    place = jnp.sum(jnp.where(chosen, places, 0), axis=3)
    used = jnp.any(chosen, axis=3)
    count = jnp.max(jnp.sum(scattered.astype(jnp.int32), axis=2), axis=1)
    same = (chain_pos // 2 % 2 == chain_pos % 2).astype(jnp.int32)
    offs = jnp.stack(
        [
            jnp.stack([jnp.int32(1), jnp.int32(2), jnp.int32(4), 3 + 2 * same]),
            jnp.stack([jnp.int32(0), jnp.int32(3), jnp.int32(5), 4 - 2 * same]),
        ]
    )
    off_inside = jnp.sum(
        jnp.where(offs[:, :, None] == slots[None, None, :], near[:, None, :].astype(jnp.int32), 0),
        axis=2,
    )
    ints = jnp.concatenate([place.reshape(2, -1), offs, count[:, None]], axis=1)
    flags = jnp.concatenate(
        [used.reshape(2, -1), centre.reshape(2, -1), off_inside == 1], axis=1
    )
    return ints, jnp.where(flags, 0.0, DEAD).astype(jnp.float32)


INT_OFFS = ROUNDS * BLOCKS_HERE
INT_COUNT = INT_OFFS + 4
BIAS_CENTRE = ROUNDS * BLOCKS_HERE
BIAS_OFF = BIAS_CENTRE + 16


def fold_rows(tile, op):
    return op(tile.reshape(BLK // 8, 8, BLK), axis=0)


def attention_kernel(
    groups_here,
    ints,
    bias,
    query,
    grad,
    own,
    partner,
    near_own,
    near_partner,
    far_own,
    far_partner,
    own_rows,
    pair_rows,
    near_back,
    far_back,
    local,
    gains,
    keys,
    keys_t,
    vals,
    vals_t,
    off_keys,
    off_vals,
    off_keys_t,
    off_vals_t,
    grad_keys,
    grad_vals,
    centre_w,
    centre_b,
    centre_d,
    off_w,
    off_b,
    off_d,
    extra_w,
    extra_b,
    out_t,
    top_rows,
    sum_rows,
    grad_scaled,
    gain_rows,
):
    windows = (own, partner, near_own, near_partner, far_own, far_partner)
    for w, ref in enumerate(windows):
        for j in range(BLOCKS_HERE):
            rows = pl.ds(j * BLK, BLK)
            key = ref[0, rows, :]
            value = ref[1, rows, :]
            keys[w * 4 + j] = key
            vals[w * 4 + j] = value
            keys_t[w * 4 + j] = key.T
            vals_t[w * 4 + j] = value.T
    gain_rows[...] = jnp.zeros_like(gain_rows)
    grad_keys[...] = jnp.zeros_like(grad_keys)
    grad_vals[...] = jnp.zeros_like(grad_vals)

    def put_rows(g, kind, i, tile):
        rows = pl.ds(i * BLK, BLK)
        if groups_here == 1:
            own_rows[kind, rows, :] = tile
            return

        @pl.when(g == 0)
        def _():
            own_rows[kind, rows, :] = tile

        @pl.when(g == 1)
        def _():
            pair_rows[kind, rows, :] = tile

    def group_task(g, carry):
        centre = g * 4
        rounds = ints[g, INT_COUNT]
        offs = [ints[g, INT_OFFS + o] * 4 for o in range(4)]

        def rows_of(i):
            return pl.ds(i * BLK, BLK)

        def gather_off(o, c):
            at = ints[g, INT_OFFS + o] * 4
            there = pl.ds(pl.multiple_of(o * BLK, BLK), BLK)
            for i in range(4):
                off_keys[i, there, :] = keys[at + i]
                off_vals[i, there, :] = vals[at + i]
                off_keys_t[i, :, there] = keys_t[at + i]
                off_vals_t[i, :, there] = vals_t[at + i]
            return c

        lax.fori_loop(0, 4, gather_off, 0)

        query_all = query[g]
        query_rows = [query[g, rows_of(i), :] for i in range(4)]
        centre_keys = keys[pl.ds(centre, 4)].reshape(TOK, HEAD_DIM)
        for i in range(4):
            off_w[i] = contract(off_keys[i], query_rows[i], 1, 1)
        centre_w[...] = contract(centre_keys, query_all, 1, 1)
        for i in range(4):
            best = None
            for j in range(4):
                part = fold_rows(centre_w[rows_of(j), rows_of(i)], jnp.max)
                part = part + bias[g, BIAS_CENTRE + i * 4 + j]
                best = part if best is None else jnp.maximum(best, part)
            for o in range(4):
                part = fold_rows(off_w[i, rows_of(o), :], jnp.max) + bias[g, BIAS_OFF + o]
                best = jnp.maximum(best, part)
            top_rows[i] = best

        def extra_scores(r, c):
            for i in range(4):
                scores = contract(keys[ints[g, r * 4 + i]], query_rows[i], 1, 1)
                extra_w[r * 4 + i] = scores
                part = fold_rows(scores, jnp.max) + bias[g, r * 4 + i]
                top_rows[i] = jnp.maximum(top_rows[i], part)
            return c

        lax.fori_loop(0, rounds, extra_scores, 0)
        tops = [jnp.max(top_rows[i], axis=0, keepdims=True) for i in range(4)]

        for i in range(4):
            total = None
            for j in range(4):
                less = tops[i] - bias[g, BIAS_CENTRE + i * 4 + j]
                weight = jnp.exp2(centre_w[rows_of(j), rows_of(i)] - less)
                centre_w[rows_of(j), rows_of(i)] = weight
                centre_b[rows_of(j), rows_of(i)] = weight.astype(jnp.bfloat16)
                part = fold_rows(weight, jnp.sum)
                total = part if total is None else total + part
            for o in range(4):
                less = tops[i] - bias[g, BIAS_OFF + o]
                weight = jnp.exp2(off_w[i, rows_of(o), :] - less)
                off_w[i, rows_of(o), :] = weight
                off_b[i, rows_of(o), :] = weight.astype(jnp.bfloat16)
                total = total + fold_rows(weight, jnp.sum)
            sum_rows[i] = total
        centre_vals_t = jnp.concatenate([vals_t[centre + j] for j in range(4)], axis=1)
        centre_out = contract(centre_vals_t, centre_b[...], 1, 0)
        for i in range(4):
            out_t[i] = centre_out[:, i * BLK : (i + 1) * BLK] + contract(
                off_vals_t[i], off_b[i], 1, 0
            )

        def extra_out(r, c):
            for i in range(4):
                less = tops[i] - bias[g, r * 4 + i]
                weight = jnp.exp2(extra_w[r * 4 + i] - less)
                extra_w[r * 4 + i] = weight
                weight_b = weight.astype(jnp.bfloat16)
                extra_b[r * 4 + i] = weight_b
                sum_rows[i] = sum_rows[i] + fold_rows(weight, jnp.sum)
                out_t[i] = out_t[i] + contract(vals_t[ints[g, r * 4 + i]], weight_b, 1, 0)
            return c

        lax.fori_loop(0, rounds, extra_out, 0)

        dots = []
        for i in range(4):
            inverse = 1.0 / jnp.sum(sum_rows[i], axis=0, keepdims=True)
            head_out = (out_t[i] * inverse).astype(jnp.bfloat16)
            put_rows(g, 0, i, head_out.T)
            grad_t = grad[g, rows_of(i), :].T.astype(jnp.float32) * inverse
            dots.append(jnp.sum(grad_t * head_out.astype(jnp.float32), axis=0, keepdims=True))
            grad_scaled[rows_of(i), :] = grad_t.astype(jnp.bfloat16).T

        grad_rows = [grad_scaled[rows_of(i), :] for i in range(4)]
        centre_vals = vals[pl.ds(centre, 4)].reshape(TOK, HEAD_DIM)
        flow = contract(centre_vals, grad_scaled[...], 1, 1)
        for i in range(4):
            for j in range(4):
                piece = flow[j * BLK : (j + 1) * BLK, i * BLK : (i + 1) * BLK]
                centre_d[rows_of(j), rows_of(i)] = (
                    centre_w[rows_of(j), rows_of(i)] * (piece - dots[i])
                ).astype(jnp.bfloat16)
            off_flow = contract(off_vals[i], grad_rows[i], 1, 1)
            for o in range(4):
                piece = off_flow[o * BLK : (o + 1) * BLK]
                off_d[i, rows_of(o), :] = (off_w[i, rows_of(o), :] * (piece - dots[i])).astype(
                    jnp.bfloat16
                )
        centre_keys_t = jnp.concatenate([keys_t[centre + j] for j in range(4)], axis=1)
        centre_grad = contract(centre_keys_t, centre_d[...], 1, 0)
        for i in range(4):
            out_t[i] = centre_grad[:, i * BLK : (i + 1) * BLK] + contract(
                off_keys_t[i], off_d[i], 1, 0
            )
        place = pl.ds(centre, 4)
        grad_keys[place] = grad_keys[place] + contract(centre_d[...], query_all, 1, 0).reshape(
            4, BLK, HEAD_DIM
        )
        grad_vals[place] = grad_vals[place] + contract(
            centre_b[...], grad_scaled[...], 1, 0
        ).reshape(4, BLK, HEAD_DIM)
        for i in range(4):
            to_keys = contract(off_d[i], query_rows[i], 1, 0)
            to_vals = contract(off_b[i], grad_rows[i], 1, 0)
            for o in range(4):
                at = offs[o] + i
                grad_keys[at] = grad_keys[at] + to_keys[o * BLK : (o + 1) * BLK]
                grad_vals[at] = grad_vals[at] + to_vals[o * BLK : (o + 1) * BLK]

        def extra_grads(r, c):
            for i in range(4):
                at = ints[g, r * 4 + i]
                piece = contract(vals[at], grad_rows[i], 1, 1)
                score_grad = (extra_w[r * 4 + i] * (piece - dots[i])).astype(jnp.bfloat16)
                out_t[i] = out_t[i] + contract(keys_t[at], score_grad, 1, 0)
                grad_keys[at] = grad_keys[at] + contract(score_grad, query_rows[i], 1, 0)
                grad_vals[at] = grad_vals[at] + contract(extra_b[r * 4 + i], grad_rows[i], 1, 0)
            return c

        lax.fori_loop(0, rounds, extra_grads, 0)
        gain_part = gain_rows[...]
        for i in range(4):
            back = (out_t[i] * SCALE).astype(jnp.bfloat16).T
            put_rows(g, 1, i, back)
            gain_part = gain_part + fold_rows(
                back.astype(jnp.float32) * query_rows[i].astype(jnp.float32), jnp.sum
            )
        gain_rows[...] = gain_part
        return carry

    lax.fori_loop(0, groups_here, group_task, 0)
    gain_sum = jnp.zeros((8, HEAD_DIM), jnp.float32)
    for n in range(WINDOWS * BLOCKS_HERE):
        gain_sum = gain_sum + fold_rows(grad_keys[n] * keys[n].astype(jnp.float32), jnp.sum)
    gains[0:1, :] = jnp.sum(gain_rows[...], axis=0, keepdims=True)
    gains[1:2, :] = jnp.sum(gain_sum, axis=0, keepdims=True)
    for n, (window, source, factor) in enumerate(
        ((1, grad_keys, LN2), (1, grad_vals, 1.0), (0, grad_keys, LN2), (0, grad_vals, 1.0))
    ):
        for j in range(BLOCKS_HERE):
            rows = pl.ds(j * BLK, BLK)
            local[n, rows, :] = source[window * 4 + j] * factor
            near_back[n, rows, :] = (source[(window + 2) * 4 + j] * factor).astype(jnp.bfloat16)
            far_back[n, rows, :] = (source[(window + 4) * 4 + j] * factor).astype(jnp.bfloat16)


def attention_slot(slot, place, groups_here, ints, bias, query, grad, windows):
    token_block = pl.BlockSpec((groups_here, TOK, HEAD_DIM), lambda n: (0, 0, place))
    window_block = pl.BlockSpec((2, TOK, HEAD_DIM), lambda n: (0, 0, slot))
    table = pl.BlockSpec(memory_space=pltpu.SMEM)
    out_token = pl.BlockSpec((2, TOK, HEAD_DIM), lambda n: (0, 0, 0))
    out_grads = pl.BlockSpec((4, TOK, HEAD_DIM), lambda n: (0, 0, 0))
    out_gains = pl.BlockSpec((2, HEAD_DIM), lambda n: (0, 0))
    tiles = WINDOWS * BLOCKS_HERE
    tile = (BLK, BLK)
    return pl.pallas_call(
        functools.partial(attention_kernel, groups_here),
        grid=(1,),
        in_specs=[table, table, token_block, token_block]
        + [window_block] * WINDOWS,
        out_specs=[out_token, out_token, out_grads, out_grads, out_grads, out_gains],
        out_shape=[
            jax.ShapeDtypeStruct((2, TOK, HEAD_DIM), jnp.bfloat16),
            jax.ShapeDtypeStruct((2, TOK, HEAD_DIM), jnp.bfloat16),
            jax.ShapeDtypeStruct((4, TOK, HEAD_DIM), jnp.bfloat16),
            jax.ShapeDtypeStruct((4, TOK, HEAD_DIM), jnp.bfloat16),
            jax.ShapeDtypeStruct((4, TOK, HEAD_DIM), jnp.float32),
            jax.ShapeDtypeStruct((2, HEAD_DIM), jnp.float32),
        ],
        scratch_shapes=[
            pltpu.VMEM((tiles,) + tile, jnp.bfloat16),
            pltpu.VMEM((tiles,) + tile, jnp.bfloat16),
            pltpu.VMEM((tiles,) + tile, jnp.bfloat16),
            pltpu.VMEM((tiles,) + tile, jnp.bfloat16),
            pltpu.VMEM((4, TOK, BLK), jnp.bfloat16),
            pltpu.VMEM((4, TOK, BLK), jnp.bfloat16),
            pltpu.VMEM((4, BLK, TOK), jnp.bfloat16),
            pltpu.VMEM((4, BLK, TOK), jnp.bfloat16),
            pltpu.VMEM((tiles,) + tile, jnp.float32),
            pltpu.VMEM((tiles,) + tile, jnp.float32),
            pltpu.VMEM((TOK, TOK), jnp.float32),
            pltpu.VMEM((TOK, TOK), jnp.bfloat16),
            pltpu.VMEM((TOK, TOK), jnp.bfloat16),
            pltpu.VMEM((4, TOK, BLK), jnp.float32),
            pltpu.VMEM((4, TOK, BLK), jnp.bfloat16),
            pltpu.VMEM((4, TOK, BLK), jnp.bfloat16),
            pltpu.VMEM((ROUNDS * 4,) + tile, jnp.float32),
            pltpu.VMEM((ROUNDS * 4,) + tile, jnp.bfloat16),
            pltpu.VMEM((4,) + tile, jnp.float32),
            pltpu.VMEM((4, 8, BLK), jnp.float32),
            pltpu.VMEM((4, 8, BLK), jnp.float32),
            pltpu.VMEM((TOK, HEAD_DIM), jnp.bfloat16),
            pltpu.VMEM((8, HEAD_DIM), jnp.float32),
        ],
        compiler_params=pltpu.CompilerParams(vmem_limit_bytes=40 * 1024 * 1024),
        cost_estimate=pl.CostEstimate(
            flops=groups_here * 40 * 6 * 2 * BLK**3 * 4,
            bytes_accessed=6 * 1024 * 1024,
            transcendentals=groups_here * 40 * BLK * BLK,
        ),
        name="attention_slot",
    )(ints, bias, query, grad, *windows)


def shards(query_raw, key_raw, values, query_gain, key_gain, out_grad, block_mask, band_strides):
    features = query_raw.shape[1]
    groups = lax.axis_size("tm")
    chain_pos = lax.axis_index("tm")
    even = chain_pos % 2 == 0
    all_features = features * lax.axis_size("head")
    half = 2 * HEAD_DIM

    def keep(x):
        return jnp.where(even, x[..., :half], x[..., half : 2 * half])

    def give(x):
        return jnp.where(even, x[..., half : 2 * half], x[..., :half])

    def last(x):
        return x[..., 2 * half :]

    query_float = query_raw.astype(jnp.float32)
    key_float = key_raw.astype(jnp.float32)
    squares = lax.psum(
        jnp.stack(
            [jnp.sum(key_float * key_float, axis=1), jnp.sum(query_float * query_float, axis=1)]
        ),
        "head",
    )
    inverses = lax.rsqrt(squares / all_features + NORM_EPSILON)
    key_inverse = inverses[0][:, None]
    query_inverse = inverses[1][:, None]
    query_unit = query_float * query_inverse
    key_unit = key_float * key_inverse
    key_normed = (key_unit * key_gain[None, :]).astype(jnp.bfloat16)

    key_values = jnp.stack([key_normed, values])
    own_keys = jnp.concatenate([keep(key_values), last(key_values)], axis=2)
    pair_keys = jnp.concatenate([give(key_values), last(key_values)], axis=2)
    partner_keys = swapped(pair_keys, "tm")
    windows = (
        own_keys,
        partner_keys,
        to_near(own_keys, "tm"),
        to_near(partner_keys, "tm"),
        to_far(own_keys, "tm"),
        to_far(partner_keys, "tm"),
    )

    query_scaled = (query_unit * (query_gain * (SCALE * LOG2E))[None, :]).astype(jnp.bfloat16)
    given_query, _ = lax.optimization_barrier(
        (jnp.stack([give(query_scaled), give(out_grad)]), partner_keys)
    )
    given = swapped(given_query, "tm")
    query_pair = jnp.stack([keep(query_scaled), given[0]])
    grad_pair = jnp.stack([keep(out_grad), given[1]])
    query_last = last(query_scaled)[None]
    grad_last = last(out_grad)[None]
    ints, bias = live_tables(chain_pos, groups, block_mask, band_strides)

    def received(result):
        return (to_near(result[2], "tm"), to_far(result[3], "tm"))

    result_last = attention_slot(2, 0, 1, ints, bias, query_last, grad_last, windows)
    received_last = received(result_last)
    result_first = attention_slot(0, 0, 2, ints, bias, query_pair, grad_pair, windows)
    received_first = received(result_first)
    rows_first = swapped(result_first[1], "tm")
    query_gated, received_last = lax.optimization_barrier((query_pair, received_last))
    result_second = attention_slot(1, 1, 2, ints, bias, query_gated, grad_pair, windows)
    received_second = received(result_second)
    rows_second = swapped(result_second[1], "tm")
    gains, rows_second = lax.optimization_barrier(
        ((result_first[5], result_second[5], result_last[5]), rows_second)
    )

    def part_sum(result, pair, start):
        stop = start + 2
        return (
            result[4][start:stop]
            + pair[0][start:stop].astype(jnp.float32)
            + pair[1][start:stop].astype(jnp.float32)
        )

    kept_grads = []
    given_grads = []
    for result, pair in (
        (result_first, received_first),
        (result_second, received_second),
        (result_last, received_last),
    ):
        back = swapped(part_sum(result, pair, 0).astype(jnp.bfloat16), "tm")
        given_grads.append(back.astype(jnp.float32))
        kept_grads.append(part_sum(result, pair, 2))

    def placed(mine, theirs, rest):
        first = jnp.where(even, mine, theirs)
        second = jnp.where(even, theirs, mine)
        return jnp.concatenate([first, second, rest], axis=-1)

    rows = placed(
        jnp.concatenate([result_first[0], result_second[0]], axis=2),
        jnp.concatenate([rows_first, rows_second], axis=2),
        result_last[0],
    )
    attended = rows[0]
    grad_query = rows[1].astype(jnp.float32)
    grads = placed(
        jnp.concatenate([kept_grads[0], kept_grads[1]], axis=2),
        jnp.concatenate([given_grads[0], given_grads[1]], axis=2),
        kept_grads[2] + given_grads[2],
    )
    grad_key = grads[0]
    grad_value = grads[1].astype(jnp.bfloat16)
    query_back = grad_query * query_gain[None, :]
    key_back = grad_key * key_gain[None, :]
    inner = lax.psum(
        jnp.stack([jnp.sum(query_back * query_unit, axis=1), jnp.sum(key_back * key_unit, axis=1)]),
        "head",
    )
    inner = inner / all_features
    query_grad = (query_inverse * (query_back - query_unit * inner[0][:, None])).astype(jnp.bfloat16)
    key_grad = (key_inverse * (key_back - key_unit * inner[1][:, None])).astype(jnp.bfloat16)
    taken = jnp.concatenate([gains[0], gains[1]], axis=1)
    gains = placed(taken, jnp.zeros_like(taken), gains[2])
    gains = gains * jnp.stack([1.0 / (query_gain * (SCALE * LOG2E)), LN2 / key_gain])
    gains = summed_over_groups(gains)
    return (attended, query_grad, key_grad, grad_value, gains[0], gains[1])


def solution(mesh):
    placed = (
        P("tm", "head"),
        P("tm", "head"),
        P("tm", "head"),
        P("head"),
        P("head"),
        P("tm", "head"),
        P(),
        P(),
    )
    return jax.shard_map(
        shards,
        mesh=mesh,
        in_specs=placed,
        out_specs=(
            P("tm", "head"),
            P("tm", "head"),
            P("tm", "head"),
            P("tm", "head"),
            P("head"),
            P("head"),
        ),
        check_vma=False,
    )
```

```python
import functools
import math

import jax
import jax.numpy as jnp
from jax import lax
from jax.experimental import pallas as pl
from jax.experimental.pallas import tpu as pltpu
from jax.sharding import PartitionSpec as P

HEAD_DIM = 128
BLK = 128
WIN = 2
BLOCKS_HERE = 4
TOK = BLK * BLOCKS_HERE
WINDOWS = 6
ROUNDS = 12
NORM_EPSILON = 1e-06
DEAD = -1e30
SCALE = 1.0 / math.sqrt(HEAD_DIM)
LOG2E = math.log2(math.e)
LN2 = math.log(2.0)


def to_near(value, axis):
    return lax.ppermute(value, axis, [(s, s ^ 2) for s in range(lax.axis_size(axis))])


def to_far(value, axis):
    count = lax.axis_size(axis)
    pairs = [(s, s - 2 if s // 2 % 2 == 0 else s + 2) for s in range(count)]
    return lax.ppermute(value, axis, [(s, d) for s, d in pairs if 0 <= d < count])


def swapped(value, axis):
    return lax.ppermute(value, axis, [(s, s ^ 1) for s in range(lax.axis_size(axis))])


def summed_over_digit(value, unit, radix):
    parts = []
    for turn in range(1, radix):
        pairs = []
        for s in range(lax.axis_size("tm")):
            digit = s // unit % radix
            pairs.append((s, s + ((digit + turn) % radix - digit) * unit))
        parts.append(lax.ppermute(value, "tm", pairs))
    for part in parts:
        value = value + part
    return value


def contract(left, right, left_dim, right_dim):
    return lax.dot_general(
        left, right, (((left_dim,), (right_dim,)), ((), ())), preferred_element_type=jnp.float32
    )


STEPS = 4 + ROUNDS
DIRECT = 2
INT_COUNT = STEPS * 4
BIAS_CENTRE = STEPS * 4


def table_kernel(chain, mask, strides, ints, bias):
    chain_pos = chain[0]
    groups = chain[1]
    partner = chain_pos ^ 1
    near_step = jnp.where(chain_pos // 2 % 2 == 0, 2, -2)
    window_groups = (
        chain_pos,
        partner,
        chain_pos + near_step,
        partner + near_step,
        chain_pos - near_step,
        partner - near_step,
    )
    same = jnp.where(chain_pos // 2 % 2 == chain_pos % 2, 1, 0)
    offs = ((1, 2, 4, 3 + 2 * same), (0, 3, 5, 4 - 2 * same))
    for g in range(2):
        query_group = window_groups[g]
        for n in range(STEPS * 4):
            ints[g, n] = 0
            bias[g, n] = jnp.float32(DEAD)
        near = []
        for w in range(WINDOWS):
            apart = jnp.abs(window_groups[w] - query_group)
            inside = (window_groups[w] >= 0) & (window_groups[w] < groups)
            near.append(jnp.where((apart <= WIN) & inside, 1, 0))
        for o in range(4):
            at = offs[g][o]
            inside = functools.reduce(
                jnp.add, [jnp.where(at == w, near[w], 0) for w in range(WINDOWS)]
            )
            for i in range(4):
                ints[g, o * 4 + i] = at * 4 + i
                bias[g, o * 4 + i] = jnp.where(inside == 1, 0.0, DEAD).astype(jnp.float32)
        counts = [jnp.int32(0)] * 4
        for w in range(WINDOWS):
            apart = window_groups[w] - query_group
            level = jnp.minimum(jnp.abs(apart), WIN)
            stride = strides[level]
            rest = lax.rem((query_group + jnp.clip(window_groups[w], 0, groups - 1)) * 4, stride)
            column = jnp.clip(apart + WIN, 0, 2 * WIN) * 4
            for i in range(4):
                row = query_group * 4 + i
                for j in range(4):
                    if w == g and i == j:
                        bias[g, BIAS_CENTRE + i * 4 + j] = jnp.float32(0.0)
                        continue
                    if i == j:
                        continue
                    total = rest + (i + j)
                    hit = functools.reduce(
                        jnp.logical_or, [total == stride * n for n in range(5)]
                    ) | (stride == 1)
                    live = (mask[row, column + j] == 1) & hit
                    if w == g:
                        bias[g, BIAS_CENTRE + i * 4 + j] = jnp.where(live, 0.0, DEAD).astype(
                            jnp.float32
                        )
                        continue
                    live = live & (near[w] == 1)

                    @pl.when(live)
                    def _(g=g, w=w, i=i, j=j, count=counts[i]):
                        ints[g, (4 + count) * 4 + i] = w * 4 + j
                        bias[g, (4 + count) * 4 + i] = jnp.float32(0.0)

                    counts[i] = counts[i] + jnp.where(live, 1, 0)
        ints[g, INT_COUNT] = functools.reduce(jnp.maximum, counts)


def live_tables(chain_pos, groups, block_mask, band_strides):
    table = pl.BlockSpec(memory_space=pltpu.SMEM)
    return pl.pallas_call(
        table_kernel,
        in_specs=[table] * 3,
        out_specs=[table] * 2,
        out_shape=[
            jax.ShapeDtypeStruct((2, INT_COUNT + 1), jnp.int32),
            jax.ShapeDtypeStruct((2, BIAS_CENTRE + 16), jnp.float32),
        ],
        name="live_tables",
    )(jnp.stack([chain_pos, jnp.int32(groups)]), block_mask, band_strides)


def fold_rows(tile, op):
    return op(tile.reshape(BLK // 8, 8, BLK), axis=0)


def attention_kernel(
    groups_here,
    ints,
    bias,
    query,
    grad,
    own_key,
    partner_key,
    near_own_key,
    near_partner_key,
    far_own_key,
    far_partner_key,
    own_value,
    partner_value,
    near_own_value,
    near_partner_value,
    far_own_value,
    far_partner_value,
    own_rows,
    pair_rows,
    near_back,
    far_back,
    local,
    gains,
    pairs,
    keys_t,
    vals_t,
    off_pairs,
    off_keys_t,
    off_vals_t,
    grads,
    centre_w,
    centre_p,
    centre_b,
    centre_d,
    off_s,
    off_d,
    extra_s,
    extra_d,
    out_t,
    top_rows,
    sum_rows,
    both,
    both_scaled,
    grad_scaled,
    gain_rows,
):
    left, right = pl.ds(0, BLK), pl.ds(BLK, BLK)
    key_windows = (
        own_key,
        partner_key,
        near_own_key,
        near_partner_key,
        far_own_key,
        far_partner_key,
    )
    value_windows = (
        own_value,
        partner_value,
        near_own_value,
        near_partner_value,
        far_own_value,
        far_partner_value,
    )
    for w in range(WINDOWS):
        for j in range(BLOCKS_HERE):
            rows = pl.ds(j * BLK, BLK)
            key = key_windows[w][rows, :]
            value = value_windows[w][rows, :]
            pairs[w * 4 + j, :, left] = key
            pairs[w * 4 + j, :, right] = value
            keys_t[w * 4 + j] = key.T
            vals_t[w * 4 + j] = value.T
    gain_rows[...] = jnp.zeros_like(gain_rows)
    grads[...] = jnp.zeros_like(grads)
    both[...] = jnp.zeros_like(both)
    both_scaled[...] = jnp.zeros_like(both_scaled)

    def put_rows(g, kind, i, tile):
        rows = pl.ds(i * BLK, BLK)
        if groups_here == 1:
            own_rows[kind, rows, :] = tile
            return

        @pl.when(g == 0)
        def _():
            own_rows[kind, rows, :] = tile

        @pl.when(g == 1)
        def _():
            pair_rows[kind, rows, :] = tile

    def rows_of(i):
        return pl.ds(i * BLK, BLK)

    def group_task(g, direct):
        centre = g * 4
        steps = 4 + direct
        all_steps = 4 + ints[g, INT_COUNT]

        def gather(s, c):
            there = pl.ds(pl.multiple_of(s * BLK, BLK), BLK)
            for i in range(4):
                at = ints[g, s * 4 + i]
                off_pairs[i, there, :] = pairs[at]
                off_keys_t[i, :, there] = keys_t[at]
                off_vals_t[i, :, there] = vals_t[at]
            return c

        lax.fori_loop(0, steps, gather, 0)
        off_span = pl.ds(0, steps * BLK)

        def loop_rest(body):
            if direct == DIRECT:
                lax.fori_loop(steps, all_steps, body, 0)

        query_all = query[g]
        grad_all = grad[g]
        for i in range(4):
            both[i, left, left] = query[g, rows_of(i), :]
            both[i, right, right] = grad[g, rows_of(i), :]
            both_scaled[i, left, left] = query[g, rows_of(i), :]
        for i in range(4):
            off_s[i, off_span, :] = contract(off_pairs[i, off_span, :], both[i], 1, 1)
        centre_keys = pairs[pl.ds(centre, 4), :, left].reshape(TOK, HEAD_DIM)
        centre_vals = pairs[pl.ds(centre, 4), :, right].reshape(TOK, HEAD_DIM)
        centre_w[...] = contract(centre_keys, query_all, 1, 1)
        centre_p[...] = contract(centre_vals, grad_all, 1, 1)
        for i in range(4):
            best = None
            for j in range(4):
                part = fold_rows(centre_w[rows_of(j), rows_of(i)], jnp.max)
                part = part + bias[g, BIAS_CENTRE + i * 4 + j]
                best = part if best is None else jnp.maximum(best, part)
            for o in range(steps):
                part = fold_rows(off_s[i, rows_of(o), left], jnp.max) + bias[g, o * 4 + i]
                best = jnp.maximum(best, part)
            top_rows[i] = best

        def rest_scores(s, c):
            for i in range(4):
                scores = contract(pairs[ints[g, s * 4 + i]], both[i], 1, 1)
                extra_s[s * 4 + i] = scores
                part = fold_rows(scores[:, :BLK], jnp.max) + bias[g, s * 4 + i]
                top_rows[i] = jnp.maximum(top_rows[i], part)
            return c

        loop_rest(rest_scores)
        tops = [jnp.max(top_rows[i], axis=0, keepdims=True) for i in range(4)]

        for i in range(4):
            total = None
            for j in range(4):
                less = tops[i] - bias[g, BIAS_CENTRE + i * 4 + j]
                weight = jnp.exp2(centre_w[rows_of(j), rows_of(i)] - less)
                centre_w[rows_of(j), rows_of(i)] = weight
                centre_b[rows_of(j), rows_of(i)] = weight.astype(jnp.bfloat16)
                part = fold_rows(weight, jnp.sum)
                total = part if total is None else total + part
            for o in range(steps):
                less = tops[i] - bias[g, o * 4 + i]
                weight = jnp.exp2(off_s[i, rows_of(o), left] - less)
                off_s[i, rows_of(o), left] = weight
                off_d[i, rows_of(o), right] = weight.astype(jnp.bfloat16)
                total = total + fold_rows(weight, jnp.sum)
            sum_rows[i] = total
        centre_vals_t = jnp.concatenate([vals_t[centre + j] for j in range(4)], axis=1)
        centre_out = contract(centre_vals_t, centre_b[...], 1, 0)
        for i in range(4):
            out_t[i] = centre_out[:, i * BLK : (i + 1) * BLK] + contract(
                off_vals_t[i, :, off_span], off_d[i, off_span, right], 1, 0
            )

        def rest_out(s, c):
            for i in range(4):
                less = tops[i] - bias[g, s * 4 + i]
                weight = jnp.exp2(extra_s[s * 4 + i, :, left] - less)
                extra_s[s * 4 + i, :, left] = weight
                weight_b = weight.astype(jnp.bfloat16)
                extra_d[s * 4 + i, :, right] = weight_b
                sum_rows[i] = sum_rows[i] + fold_rows(weight, jnp.sum)
                out_t[i] = out_t[i] + contract(vals_t[ints[g, s * 4 + i]], weight_b, 1, 0)
            return c

        loop_rest(rest_out)

        dots = []
        inverses = []
        for i in range(4):
            inverse = 1.0 / jnp.sum(sum_rows[i], axis=0, keepdims=True)
            head_out = (out_t[i] * inverse).astype(jnp.bfloat16)
            put_rows(g, 0, i, head_out.T)
            grad_t = grad[g, rows_of(i), :].T.astype(jnp.float32) * inverse
            dots.append(jnp.sum(grad_t * head_out.astype(jnp.float32), axis=0, keepdims=True))
            inverses.append(inverse)
            scaled = grad_t.astype(jnp.bfloat16).T
            grad_scaled[rows_of(i), :] = scaled
            both_scaled[i, right, right] = scaled

        for i in range(4):
            for j in range(4):
                flow = centre_p[rows_of(j), rows_of(i)] * inverses[i] - dots[i]
                centre_d[rows_of(j), rows_of(i)] = (
                    centre_w[rows_of(j), rows_of(i)] * flow
                ).astype(jnp.bfloat16)
            for o in range(steps):
                flow = off_s[i, rows_of(o), right] * inverses[i] - dots[i]
                off_d[i, rows_of(o), left] = (off_s[i, rows_of(o), left] * flow).astype(
                    jnp.bfloat16
                )
        centre_keys_t = jnp.concatenate([keys_t[centre + j] for j in range(4)], axis=1)
        centre_grad = contract(centre_keys_t, centre_d[...], 1, 0)
        for i in range(4):
            out_t[i] = centre_grad[:, i * BLK : (i + 1) * BLK] + contract(
                off_keys_t[i, :, off_span], off_d[i, off_span, left], 1, 0
            )
        place = pl.ds(centre, 4)
        grads[place, :, left] = grads[place, :, left] + contract(
            centre_d[...], query_all, 1, 0
        ).reshape(4, BLK, HEAD_DIM)
        grads[place, :, right] = grads[place, :, right] + contract(
            centre_b[...], grad_scaled[...], 1, 0
        ).reshape(4, BLK, HEAD_DIM)
        for i in range(4):
            part = contract(off_d[i, off_span, :], both_scaled[i], 1, 0)
            for o in range(steps):
                at = ints[g, o * 4 + i]
                grads[at] = grads[at] + part[o * BLK : (o + 1) * BLK]

        def rest_grads(s, c):
            for i in range(4):
                at = ints[g, s * 4 + i]
                flow = extra_s[s * 4 + i, :, right] * inverses[i] - dots[i]
                score_grad = (extra_s[s * 4 + i, :, left] * flow).astype(jnp.bfloat16)
                extra_d[s * 4 + i, :, left] = score_grad
                out_t[i] = out_t[i] + contract(keys_t[at], score_grad, 1, 0)
                grads[at] = grads[at] + contract(extra_d[s * 4 + i], both_scaled[i], 1, 0)
            return c

        loop_rest(rest_grads)
        gain_part = gain_rows[...]
        for i in range(4):
            back = (out_t[i] * SCALE).astype(jnp.bfloat16).T
            put_rows(g, 1, i, back)
            gain_part = gain_part + fold_rows(
                back.astype(jnp.float32) * query[g, rows_of(i), :].astype(jnp.float32), jnp.sum
            )
        gain_rows[...] = gain_part

    def any_task(g, carry):
        group_task(g, DIRECT)
        return carry

    lax.fori_loop(0, groups_here, any_task, 0)
    gain_sum = jnp.zeros((8, HEAD_DIM), jnp.float32)
    for n in range(WINDOWS * BLOCKS_HERE):
        gain_sum = gain_sum + fold_rows(
            grads[n, :, left] * pairs[n, :, left].astype(jnp.float32), jnp.sum
        )
    gains[0:1, :] = jnp.sum(gain_rows[...], axis=0, keepdims=True)
    gains[1:2, :] = jnp.sum(gain_sum, axis=0, keepdims=True)
    for n, (window, half, factor) in enumerate(
        ((1, left, LN2), (1, right, 1.0), (0, left, LN2), (0, right, 1.0))
    ):
        for j in range(BLOCKS_HERE):
            rows = pl.ds(j * BLK, BLK)
            local[n, rows, :] = grads[window * 4 + j, :, half] * factor
            near_back[n, rows, :] = (grads[(window + 2) * 4 + j, :, half] * factor).astype(
                jnp.bfloat16
            )
            far_back[n, rows, :] = (grads[(window + 4) * 4 + j, :, half] * factor).astype(
                jnp.bfloat16
            )


def attention_slot(slot, place, groups_here, ints, bias, query, grad, windows):
    token_block = pl.BlockSpec((groups_here, TOK, HEAD_DIM), lambda n: (0, 0, place))
    window_block = pl.BlockSpec((TOK, HEAD_DIM), lambda n: (0, slot))
    table = pl.BlockSpec(memory_space=pltpu.SMEM)
    out_token = pl.BlockSpec((2, TOK, HEAD_DIM), lambda n: (0, 0, 0))
    out_grads = pl.BlockSpec((4, TOK, HEAD_DIM), lambda n: (0, 0, 0))
    out_gains = pl.BlockSpec((2, HEAD_DIM), lambda n: (0, 0))
    tiles = WINDOWS * BLOCKS_HERE
    most = 4 + DIRECT
    return pl.pallas_call(
        functools.partial(attention_kernel, groups_here),
        grid=(1,),
        in_specs=[table, table, token_block, token_block]
        + [window_block] * (2 * WINDOWS),
        out_specs=[out_token, out_token, out_grads, out_grads, out_grads, out_gains],
        out_shape=[
            jax.ShapeDtypeStruct((2, TOK, HEAD_DIM), jnp.bfloat16),
            jax.ShapeDtypeStruct((2, TOK, HEAD_DIM), jnp.bfloat16),
            jax.ShapeDtypeStruct((4, TOK, HEAD_DIM), jnp.bfloat16),
            jax.ShapeDtypeStruct((4, TOK, HEAD_DIM), jnp.bfloat16),
            jax.ShapeDtypeStruct((4, TOK, HEAD_DIM), jnp.float32),
            jax.ShapeDtypeStruct((2, HEAD_DIM), jnp.float32),
        ],
        scratch_shapes=[
            pltpu.VMEM((tiles, BLK, 2 * BLK), jnp.bfloat16),
            pltpu.VMEM((tiles, BLK, BLK), jnp.bfloat16),
            pltpu.VMEM((tiles, BLK, BLK), jnp.bfloat16),
            pltpu.VMEM((4, most * BLK, 2 * BLK), jnp.bfloat16),
            pltpu.VMEM((4, BLK, most * BLK), jnp.bfloat16),
            pltpu.VMEM((4, BLK, most * BLK), jnp.bfloat16),
            pltpu.VMEM((tiles, BLK, 2 * BLK), jnp.float32),
            pltpu.VMEM((TOK, TOK), jnp.float32),
            pltpu.VMEM((TOK, TOK), jnp.float32),
            pltpu.VMEM((TOK, TOK), jnp.bfloat16),
            pltpu.VMEM((TOK, TOK), jnp.bfloat16),
            pltpu.VMEM((4, most * BLK, 2 * BLK), jnp.float32),
            pltpu.VMEM((4, most * BLK, 2 * BLK), jnp.bfloat16),
            pltpu.VMEM((STEPS * 4, BLK, 2 * BLK), jnp.float32),
            pltpu.VMEM((STEPS * 4, BLK, 2 * BLK), jnp.bfloat16),
            pltpu.VMEM((4, BLK, BLK), jnp.float32),
            pltpu.VMEM((4, 8, BLK), jnp.float32),
            pltpu.VMEM((4, 8, BLK), jnp.float32),
            pltpu.VMEM((4, 2 * BLK, 2 * BLK), jnp.bfloat16),
            pltpu.VMEM((4, 2 * BLK, 2 * BLK), jnp.bfloat16),
            pltpu.VMEM((TOK, HEAD_DIM), jnp.bfloat16),
            pltpu.VMEM((8, HEAD_DIM), jnp.float32),
        ],
        compiler_params=pltpu.CompilerParams(vmem_limit_bytes=40 * 1024 * 1024),
        cost_estimate=pl.CostEstimate(
            flops=groups_here * 40 * 6 * 2 * BLK**3 * 4,
            bytes_accessed=6 * 1024 * 1024,
            transcendentals=groups_here * 40 * BLK * BLK,
        ),
        name="attention_slot",
    )(ints, bias, query, grad, *windows)


def shards(query_raw, key_raw, values, query_gain, key_gain, out_grad, block_mask, band_strides):
    features = query_raw.shape[1]
    groups = lax.axis_size("tm")
    chain_pos = lax.axis_index("tm")
    even = chain_pos % 2 == 0
    all_features = features * lax.axis_size("head")
    half = 2 * HEAD_DIM

    def keep(x):
        return jnp.where(even, x[..., :half], x[..., half : 2 * half])

    def give(x):
        return jnp.where(even, x[..., half : 2 * half], x[..., :half])

    def last(x):
        return x[..., 2 * half :]

    def spread(rows, ahead=()):
        own = jnp.concatenate([keep(rows), last(rows)], axis=1)
        partner = swapped(jnp.concatenate([give(rows), last(rows)], axis=1), "tm")
        near_own, far_own = to_near(own, "tm"), to_far(own, "tm")
        partner, _ = lax.optimization_barrier((partner, ahead))
        near_partner, far_partner = to_near(partner, "tm"), to_far(partner, "tm")
        return (own, partner, near_own, near_partner, far_own, far_partner)

    value_windows = spread(values)
    query_float = query_raw.astype(jnp.float32)
    key_float = key_raw.astype(jnp.float32)
    shares = jnp.stack(
        [jnp.sum(key_float * key_float, axis=1), jnp.sum(query_float * query_float, axis=1)]
    )
    squares = lax.psum(shares, "head")
    inverses = lax.rsqrt(squares / all_features + NORM_EPSILON)
    key_inverse = inverses[0][:, None]
    query_inverse = inverses[1][:, None]
    query_unit = query_float * query_inverse
    key_unit = key_float * key_inverse
    key_normed = (key_unit * key_gain[None, :]).astype(jnp.bfloat16)
    key_windows = spread(key_normed, value_windows[2:5:2])
    windows = lax.optimization_barrier(key_windows + value_windows)

    query_scaled = (query_unit * (query_gain * (SCALE * LOG2E))[None, :]).astype(jnp.bfloat16)
    given_query, _ = lax.optimization_barrier(
        (jnp.stack([give(query_scaled), give(out_grad)]), key_windows[1])
    )
    given = swapped(given_query, "tm")
    query_pair = jnp.stack([keep(query_scaled), given[0]])
    grad_pair = jnp.stack([keep(out_grad), given[1]])
    query_last = last(query_scaled)[None]
    grad_last = last(out_grad)[None]
    ints, bias = live_tables(chain_pos, groups, block_mask, band_strides)

    def received(result):
        return (to_near(result[2], "tm"), to_far(result[3], "tm"))

    result_last = attention_slot(2, 0, 1, ints, bias, query_last, grad_last, windows)
    received_last = received(result_last)
    result_first = attention_slot(0, 0, 2, ints, bias, query_pair, grad_pair, windows)
    received_first = received(result_first)
    query_gated, rows_to_give, received_last = lax.optimization_barrier(
        (query_pair, result_first[1], received_last)
    )
    rows_first = swapped(rows_to_give, "tm")
    result_second = attention_slot(1, 1, 2, ints, bias, query_gated, grad_pair, windows)
    received_second = received(result_second)
    gains = (result_first[5], result_second[5], result_last[5])

    def placed(mine, theirs, rest):
        first = jnp.where(even, mine, theirs)
        second = jnp.where(even, theirs, mine)
        return jnp.concatenate([first, second, rest], axis=-1)

    taken = jnp.concatenate([gains[0], gains[1]], axis=1)
    gains = placed(taken, jnp.zeros_like(taken), gains[2])
    gains = gains * jnp.stack([1.0 / (query_gain * (SCALE * LOG2E)), LN2 / key_gain])
    gains = summed_over_digit(gains, 1, 2)

    def part_sum(result, pair, start):
        stop = start + 2
        return (
            result[4][start:stop]
            + pair[0][start:stop].astype(jnp.float32)
            + pair[1][start:stop].astype(jnp.float32)
        )

    results = (result_first, result_second, result_last)
    give_first, give_last = (
        part_sum(result, pair, 0).astype(jnp.bfloat16)
        for result, pair in ((result_first, received_first), (result_last, received_last))
    )
    gains, rows_to_give, give_first, give_last = lax.optimization_barrier(
        (gains, result_second[1], give_first, give_last)
    )
    rows_second = swapped(rows_to_give, "tm")
    gains, rows_second = lax.optimization_barrier((gains, rows_second))
    gains = summed_over_digit(gains, 2, 4)
    give_second = part_sum(result_second, received_second, 0).astype(jnp.bfloat16)
    pairs = (received_first, received_second, received_last)
    kept_grads = [part_sum(result, pair, 2) for result, pair in zip(results, pairs)]
    given_grads = [
        swapped(part, "tm").astype(jnp.float32) for part in (give_first, give_second, give_last)
    ]
    gains, given_grads = lax.optimization_barrier((gains, given_grads))
    gains = summed_over_digit(gains, 8, 4)

    rows = placed(
        jnp.concatenate([result_first[0], result_second[0]], axis=2),
        jnp.concatenate([rows_first, rows_second], axis=2),
        result_last[0],
    )
    attended = rows[0]
    grad_query = rows[1].astype(jnp.float32)
    grads = placed(
        jnp.concatenate([kept_grads[0], kept_grads[1]], axis=2),
        jnp.concatenate([given_grads[0], given_grads[1]], axis=2),
        kept_grads[2] + given_grads[2],
    )
    grad_key = grads[0]
    grad_value = grads[1].astype(jnp.bfloat16)
    query_back = grad_query * query_gain[None, :]
    key_back = grad_key * key_gain[None, :]
    inner = lax.psum(
        jnp.stack([jnp.sum(query_back * query_unit, axis=1), jnp.sum(key_back * key_unit, axis=1)]),
        "head",
    )
    inner = inner / all_features
    query_grad = (query_inverse * (query_back - query_unit * inner[0][:, None])).astype(jnp.bfloat16)
    key_grad = (key_inverse * (key_back - key_unit * inner[1][:, None])).astype(jnp.bfloat16)
    return (attended, query_grad, key_grad, grad_value, gains[0], gains[1])


def solution(mesh):
    placed = (
        P("tm", "head"),
        P("tm", "head"),
        P("tm", "head"),
        P("head"),
        P("head"),
        P("tm", "head"),
        P(),
        P(),
    )
    return jax.shard_map(
        shards,
        mesh=mesh,
        in_specs=placed,
        out_specs=(
            P("tm", "head"),
            P("tm", "head"),
            P("tm", "head"),
            P("tm", "head"),
            P("head"),
            P("head"),
        ),
        check_vma=False,
    )
```

```python
import functools
import math

import jax
import jax.numpy as jnp
from jax import lax
from jax.experimental import pallas as pl
from jax.experimental.pallas import tpu as pltpu
from jax.sharding import PartitionSpec as P

HEAD_DIM = 128
BLK = 128
WIN = 2
BLOCKS_HERE = 4
TOK = BLK * BLOCKS_HERE
WINDOWS = 6
ROUNDS = 12
NORM_EPSILON = 1e-06
DEAD = -1e30
SCALE = 1.0 / math.sqrt(HEAD_DIM)
LOG2E = math.log2(math.e)
LN2 = math.log(2.0)


def to_near(value, axis):
    return lax.ppermute(value, axis, [(s, s ^ 2) for s in range(lax.axis_size(axis))])


def to_far(value, axis):
    count = lax.axis_size(axis)
    pairs = [(s, s - 2 if s // 2 % 2 == 0 else s + 2) for s in range(count)]
    return lax.ppermute(value, axis, [(s, d) for s, d in pairs if 0 <= d < count])


def swapped(value, axis):
    return lax.ppermute(value, axis, [(s, s ^ 1) for s in range(lax.axis_size(axis))])


def summed_over_digit(value, unit, radix):
    parts = []
    for turn in range(1, radix):
        pairs = []
        for s in range(lax.axis_size("tm")):
            digit = s // unit % radix
            pairs.append((s, s + ((digit + turn) % radix - digit) * unit))
        parts.append(lax.ppermute(value, "tm", pairs))
    for part in parts:
        value = value + part
    return value


def contract(left, right, left_dim, right_dim):
    return lax.dot_general(
        left, right, (((left_dim,), (right_dim,)), ((), ())), preferred_element_type=jnp.float32
    )


STEPS = 4 + ROUNDS
DIRECT = 1
INT_COUNT = STEPS * 4
BIAS_CENTRE = STEPS * 4


def table_kernel(chain, mask, strides, ints, bias):
    chain_pos = chain[0]
    groups = chain[1]
    partner = chain_pos ^ 1
    near_step = jnp.where(chain_pos // 2 % 2 == 0, 2, -2)
    window_groups = (
        chain_pos,
        partner,
        chain_pos + near_step,
        partner + near_step,
        chain_pos - near_step,
        partner - near_step,
    )
    same = jnp.where(chain_pos // 2 % 2 == chain_pos % 2, 1, 0)
    offs = ((1, 2, 4, 3 + 2 * same), (0, 3, 5, 4 - 2 * same))
    for g in range(2):
        query_group = window_groups[g]
        for n in range(STEPS * 4):
            ints[g, n] = 0
            bias[g, n] = jnp.float32(DEAD)
        near = []
        for w in range(WINDOWS):
            apart = jnp.abs(window_groups[w] - query_group)
            inside = (window_groups[w] >= 0) & (window_groups[w] < groups)
            near.append(jnp.where((apart <= WIN) & inside, 1, 0))
        for o in range(4):
            at = offs[g][o]
            inside = functools.reduce(
                jnp.add, [jnp.where(at == w, near[w], 0) for w in range(WINDOWS)]
            )
            for i in range(4):
                ints[g, o * 4 + i] = at * 4 + i
                bias[g, o * 4 + i] = jnp.where(inside == 1, 0.0, DEAD).astype(jnp.float32)
        counts = [jnp.int32(0)] * 4
        for w in range(WINDOWS):
            apart = window_groups[w] - query_group
            level = jnp.minimum(jnp.abs(apart), WIN)
            stride = strides[level]
            rest = lax.rem((query_group + jnp.clip(window_groups[w], 0, groups - 1)) * 4, stride)
            column = jnp.clip(apart + WIN, 0, 2 * WIN) * 4
            for i in range(4):
                row = query_group * 4 + i
                for j in range(4):
                    if w == g and i == j:
                        bias[g, BIAS_CENTRE + i * 4 + j] = jnp.float32(0.0)
                        continue
                    if i == j:
                        continue
                    total = rest + (i + j)
                    hit = functools.reduce(
                        jnp.logical_or, [total == stride * n for n in range(5)]
                    ) | (stride == 1)
                    live = (mask[row, column + j] == 1) & hit
                    if w == g:
                        bias[g, BIAS_CENTRE + i * 4 + j] = jnp.where(live, 0.0, DEAD).astype(
                            jnp.float32
                        )
                        continue
                    live = live & (near[w] == 1)

                    @pl.when(live)
                    def _(g=g, w=w, i=i, j=j, count=counts[i]):
                        ints[g, (4 + count) * 4 + i] = w * 4 + j
                        bias[g, (4 + count) * 4 + i] = jnp.float32(0.0)

                    counts[i] = counts[i] + jnp.where(live, 1, 0)
        ints[g, INT_COUNT] = functools.reduce(jnp.maximum, counts)


def live_tables(chain_pos, groups, block_mask, band_strides):
    table = pl.BlockSpec(memory_space=pltpu.SMEM)
    return pl.pallas_call(
        table_kernel,
        in_specs=[table] * 3,
        out_specs=[table] * 2,
        out_shape=[
            jax.ShapeDtypeStruct((2, INT_COUNT + 1), jnp.int32),
            jax.ShapeDtypeStruct((2, BIAS_CENTRE + 16), jnp.float32),
        ],
        name="live_tables",
    )(jnp.stack([chain_pos, jnp.int32(groups)]), block_mask, band_strides)


def fold_rows(tile, op):
    return op(tile.reshape(BLK // 8, 8, BLK), axis=0)


def attention_kernel(
    groups_here,
    ints,
    bias,
    query,
    grad,
    own_key,
    partner_key,
    near_own_key,
    near_partner_key,
    far_own_key,
    far_partner_key,
    own_value,
    partner_value,
    near_own_value,
    near_partner_value,
    far_own_value,
    far_partner_value,
    own_rows,
    pair_rows,
    near_back,
    far_back,
    local,
    gains,
    pairs,
    keys_t,
    vals_t,
    off_pairs,
    off_keys_t,
    off_vals_t,
    grads,
    centre_w,
    centre_p,
    centre_b,
    centre_d,
    off_s,
    off_d,
    extra_s,
    extra_d,
    out_t,
    top_rows,
    sum_rows,
    both,
    both_scaled,
    grad_scaled,
    gain_rows,
):
    left, right = pl.ds(0, BLK), pl.ds(BLK, BLK)
    key_windows = (
        own_key,
        partner_key,
        near_own_key,
        near_partner_key,
        far_own_key,
        far_partner_key,
    )
    value_windows = (
        own_value,
        partner_value,
        near_own_value,
        near_partner_value,
        far_own_value,
        far_partner_value,
    )
    for w in range(WINDOWS):
        for j in range(BLOCKS_HERE):
            rows = pl.ds(j * BLK, BLK)
            key = key_windows[w][rows, :]
            value = value_windows[w][rows, :]
            pairs[w * 4 + j, :, left] = key
            pairs[w * 4 + j, :, right] = value
            keys_t[w * 4 + j] = key.T
            vals_t[w * 4 + j] = value.T
    gain_rows[...] = jnp.zeros_like(gain_rows)
    grads[...] = jnp.zeros_like(grads)
    both[...] = jnp.zeros_like(both)
    both_scaled[...] = jnp.zeros_like(both_scaled)

    def put_rows(g, kind, i, tile):
        rows = pl.ds(i * BLK, BLK)
        if groups_here == 1:
            own_rows[kind, rows, :] = tile
            return

        @pl.when(g == 0)
        def _():
            own_rows[kind, rows, :] = tile

        @pl.when(g == 1)
        def _():
            pair_rows[kind, rows, :] = tile

    def rows_of(i):
        return pl.ds(i * BLK, BLK)

    def group_task(g, direct):
        centre = g * 4
        steps = 4 + direct
        all_steps = 4 + ints[g, INT_COUNT]

        def gather(s, c):
            there = pl.ds(pl.multiple_of(s * BLK, BLK), BLK)
            for i in range(4):
                at = ints[g, s * 4 + i]
                off_pairs[i, there, :] = pairs[at]
                off_keys_t[i, :, there] = keys_t[at]
                off_vals_t[i, :, there] = vals_t[at]
            return c

        lax.fori_loop(0, steps, gather, 0)
        off_span = pl.ds(0, steps * BLK)

        def loop_rest(body):
            if direct == DIRECT:
                lax.fori_loop(steps, all_steps, body, 0)

        query_all = query[g]
        grad_all = grad[g]
        for i in range(4):
            both[i, left, left] = query[g, rows_of(i), :]
            both[i, right, right] = grad[g, rows_of(i), :]
            both_scaled[i, left, left] = query[g, rows_of(i), :]
        for i in range(4):
            off_s[i, off_span, :] = contract(off_pairs[i, off_span, :], both[i], 1, 1)
        centre_keys = pairs[pl.ds(centre, 4), :, left].reshape(TOK, HEAD_DIM)
        centre_vals = pairs[pl.ds(centre, 4), :, right].reshape(TOK, HEAD_DIM)
        centre_w[...] = contract(centre_keys, query_all, 1, 1)
        centre_p[...] = contract(centre_vals, grad_all, 1, 1)
        for i in range(4):
            best = None
            for j in range(4):
                part = fold_rows(centre_w[rows_of(j), rows_of(i)], jnp.max)
                part = part + bias[g, BIAS_CENTRE + i * 4 + j]
                best = part if best is None else jnp.maximum(best, part)
            for o in range(steps):
                part = fold_rows(off_s[i, rows_of(o), left], jnp.max) + bias[g, o * 4 + i]
                best = jnp.maximum(best, part)
            top_rows[i] = best

        def rest_scores(s, c):
            for i in range(4):
                scores = contract(pairs[ints[g, s * 4 + i]], both[i], 1, 1)
                extra_s[s * 4 + i] = scores
                part = fold_rows(scores[:, :BLK], jnp.max) + bias[g, s * 4 + i]
                top_rows[i] = jnp.maximum(top_rows[i], part)
            return c

        loop_rest(rest_scores)
        tops = [jnp.max(top_rows[i], axis=0, keepdims=True) for i in range(4)]

        for i in range(4):
            total = None
            for j in range(4):
                less = tops[i] - bias[g, BIAS_CENTRE + i * 4 + j]
                weight = jnp.exp2(centre_w[rows_of(j), rows_of(i)] - less)
                centre_w[rows_of(j), rows_of(i)] = weight
                centre_b[rows_of(j), rows_of(i)] = weight.astype(jnp.bfloat16)
                part = fold_rows(weight, jnp.sum)
                total = part if total is None else total + part
            for o in range(steps):
                less = tops[i] - bias[g, o * 4 + i]
                weight = jnp.exp2(off_s[i, rows_of(o), left] - less)
                off_s[i, rows_of(o), left] = weight
                off_d[i, rows_of(o), right] = weight.astype(jnp.bfloat16)
                total = total + fold_rows(weight, jnp.sum)
            sum_rows[i] = total
        centre_vals_t = jnp.concatenate([vals_t[centre + j] for j in range(4)], axis=1)
        centre_out = contract(centre_vals_t, centre_b[...], 1, 0)
        for i in range(4):
            out_t[i] = centre_out[:, i * BLK : (i + 1) * BLK] + contract(
                off_vals_t[i, :, off_span], off_d[i, off_span, right], 1, 0
            )

        def rest_out(s, c):
            for i in range(4):
                less = tops[i] - bias[g, s * 4 + i]
                weight = jnp.exp2(extra_s[s * 4 + i, :, left] - less)
                extra_s[s * 4 + i, :, left] = weight
                weight_b = weight.astype(jnp.bfloat16)
                extra_d[s * 4 + i, :, right] = weight_b
                sum_rows[i] = sum_rows[i] + fold_rows(weight, jnp.sum)
                out_t[i] = out_t[i] + contract(vals_t[ints[g, s * 4 + i]], weight_b, 1, 0)
            return c

        loop_rest(rest_out)

        dots = []
        inverses = []
        for i in range(4):
            inverse = 1.0 / jnp.sum(sum_rows[i], axis=0, keepdims=True)
            head_out = (out_t[i] * inverse).astype(jnp.bfloat16)
            put_rows(g, 0, i, head_out.T)
            grad_t = grad[g, rows_of(i), :].T.astype(jnp.float32) * inverse
            dots.append(jnp.sum(grad_t * head_out.astype(jnp.float32), axis=0, keepdims=True))
            inverses.append(inverse)
            scaled = grad_t.astype(jnp.bfloat16).T
            grad_scaled[rows_of(i), :] = scaled
            both_scaled[i, right, right] = scaled

        for i in range(4):
            for j in range(4):
                flow = centre_p[rows_of(j), rows_of(i)] * inverses[i] - dots[i]
                centre_d[rows_of(j), rows_of(i)] = (
                    centre_w[rows_of(j), rows_of(i)] * flow
                ).astype(jnp.bfloat16)
            for o in range(steps):
                flow = off_s[i, rows_of(o), right] * inverses[i] - dots[i]
                off_d[i, rows_of(o), left] = (off_s[i, rows_of(o), left] * flow).astype(
                    jnp.bfloat16
                )
        centre_keys_t = jnp.concatenate([keys_t[centre + j] for j in range(4)], axis=1)
        centre_grad = contract(centre_keys_t, centre_d[...], 1, 0)
        for i in range(4):
            out_t[i] = centre_grad[:, i * BLK : (i + 1) * BLK] + contract(
                off_keys_t[i, :, off_span], off_d[i, off_span, left], 1, 0
            )
        place = pl.ds(centre, 4)
        grads[place, :, left] = grads[place, :, left] + contract(
            centre_d[...], query_all, 1, 0
        ).reshape(4, BLK, HEAD_DIM)
        grads[place, :, right] = grads[place, :, right] + contract(
            centre_b[...], grad_scaled[...], 1, 0
        ).reshape(4, BLK, HEAD_DIM)
        for i in range(4):
            part = contract(off_d[i, off_span, :], both_scaled[i], 1, 0)
            for o in range(steps):
                at = ints[g, o * 4 + i]
                grads[at] = grads[at] + part[o * BLK : (o + 1) * BLK]

        def rest_grads(s, c):
            for i in range(4):
                at = ints[g, s * 4 + i]
                flow = extra_s[s * 4 + i, :, right] * inverses[i] - dots[i]
                score_grad = (extra_s[s * 4 + i, :, left] * flow).astype(jnp.bfloat16)
                extra_d[s * 4 + i, :, left] = score_grad
                out_t[i] = out_t[i] + contract(keys_t[at], score_grad, 1, 0)
                grads[at] = grads[at] + contract(extra_d[s * 4 + i], both_scaled[i], 1, 0)
            return c

        loop_rest(rest_grads)
        gain_part = gain_rows[...]
        for i in range(4):
            back = (out_t[i] * SCALE).astype(jnp.bfloat16).T
            put_rows(g, 1, i, back)
            gain_part = gain_part + fold_rows(
                back.astype(jnp.float32) * query[g, rows_of(i), :].astype(jnp.float32), jnp.sum
            )
        gain_rows[...] = gain_part

    def any_task(g, carry):
        group_task(g, DIRECT)
        return carry

    lax.fori_loop(0, groups_here, any_task, 0)
    gain_sum = jnp.zeros((8, HEAD_DIM), jnp.float32)
    for n in range(WINDOWS * BLOCKS_HERE):
        gain_sum = gain_sum + fold_rows(
            grads[n, :, left] * pairs[n, :, left].astype(jnp.float32), jnp.sum
        )
    gains[0:1, :] = jnp.sum(gain_rows[...], axis=0, keepdims=True)
    gains[1:2, :] = jnp.sum(gain_sum, axis=0, keepdims=True)
    for n, (window, half, factor) in enumerate(
        ((1, left, LN2), (1, right, 1.0), (0, left, LN2), (0, right, 1.0))
    ):
        for j in range(BLOCKS_HERE):
            rows = pl.ds(j * BLK, BLK)
            local[n, rows, :] = grads[window * 4 + j, :, half] * factor
            near_back[n, rows, :] = (grads[(window + 2) * 4 + j, :, half] * factor).astype(
                jnp.bfloat16
            )
            far_back[n, rows, :] = (grads[(window + 4) * 4 + j, :, half] * factor).astype(
                jnp.bfloat16
            )


def attention_slot(slot, place, groups_here, ints, bias, query, grad, windows):
    token_block = pl.BlockSpec((groups_here, TOK, HEAD_DIM), lambda n: (0, 0, place))
    window_block = pl.BlockSpec((TOK, HEAD_DIM), lambda n: (0, slot))
    table = pl.BlockSpec(memory_space=pltpu.SMEM)
    out_token = pl.BlockSpec((2, TOK, HEAD_DIM), lambda n: (0, 0, 0))
    out_grads = pl.BlockSpec((4, TOK, HEAD_DIM), lambda n: (0, 0, 0))
    out_gains = pl.BlockSpec((2, HEAD_DIM), lambda n: (0, 0))
    tiles = WINDOWS * BLOCKS_HERE
    most = 4 + DIRECT
    return pl.pallas_call(
        functools.partial(attention_kernel, groups_here),
        grid=(1,),
        in_specs=[table, table, token_block, token_block]
        + [window_block] * (2 * WINDOWS),
        out_specs=[out_token, out_token, out_grads, out_grads, out_grads, out_gains],
        out_shape=[
            jax.ShapeDtypeStruct((2, TOK, HEAD_DIM), jnp.bfloat16),
            jax.ShapeDtypeStruct((2, TOK, HEAD_DIM), jnp.bfloat16),
            jax.ShapeDtypeStruct((4, TOK, HEAD_DIM), jnp.bfloat16),
            jax.ShapeDtypeStruct((4, TOK, HEAD_DIM), jnp.bfloat16),
            jax.ShapeDtypeStruct((4, TOK, HEAD_DIM), jnp.float32),
            jax.ShapeDtypeStruct((2, HEAD_DIM), jnp.float32),
        ],
        scratch_shapes=[
            pltpu.VMEM((tiles, BLK, 2 * BLK), jnp.bfloat16),
            pltpu.VMEM((tiles, BLK, BLK), jnp.bfloat16),
            pltpu.VMEM((tiles, BLK, BLK), jnp.bfloat16),
            pltpu.VMEM((4, most * BLK, 2 * BLK), jnp.bfloat16),
            pltpu.VMEM((4, BLK, most * BLK), jnp.bfloat16),
            pltpu.VMEM((4, BLK, most * BLK), jnp.bfloat16),
            pltpu.VMEM((tiles, BLK, 2 * BLK), jnp.float32),
            pltpu.VMEM((TOK, TOK), jnp.float32),
            pltpu.VMEM((TOK, TOK), jnp.float32),
            pltpu.VMEM((TOK, TOK), jnp.bfloat16),
            pltpu.VMEM((TOK, TOK), jnp.bfloat16),
            pltpu.VMEM((4, most * BLK, 2 * BLK), jnp.float32),
            pltpu.VMEM((4, most * BLK, 2 * BLK), jnp.bfloat16),
            pltpu.VMEM((STEPS * 4, BLK, 2 * BLK), jnp.float32),
            pltpu.VMEM((STEPS * 4, BLK, 2 * BLK), jnp.bfloat16),
            pltpu.VMEM((4, BLK, BLK), jnp.float32),
            pltpu.VMEM((4, 8, BLK), jnp.float32),
            pltpu.VMEM((4, 8, BLK), jnp.float32),
            pltpu.VMEM((4, 2 * BLK, 2 * BLK), jnp.bfloat16),
            pltpu.VMEM((4, 2 * BLK, 2 * BLK), jnp.bfloat16),
            pltpu.VMEM((TOK, HEAD_DIM), jnp.bfloat16),
            pltpu.VMEM((8, HEAD_DIM), jnp.float32),
        ],
        compiler_params=pltpu.CompilerParams(vmem_limit_bytes=40 * 1024 * 1024),
        cost_estimate=pl.CostEstimate(
            flops=groups_here * 40 * 6 * 2 * BLK**3 * 4,
            bytes_accessed=6 * 1024 * 1024,
            transcendentals=groups_here * 40 * BLK * BLK,
        ),
        name="attention_slot",
    )(ints, bias, query, grad, *windows)


def shards(query_raw, key_raw, values, query_gain, key_gain, out_grad, block_mask, band_strides):
    features = query_raw.shape[1]
    groups = lax.axis_size("tm")
    chain_pos = lax.axis_index("tm")
    even = chain_pos % 2 == 0
    all_features = features * lax.axis_size("head")
    half = 2 * HEAD_DIM

    def keep(x):
        return jnp.where(even, x[..., :half], x[..., half : 2 * half])

    def give(x):
        return jnp.where(even, x[..., half : 2 * half], x[..., :half])

    def last(x):
        return x[..., 2 * half :]

    def spread(rows, ahead=()):
        own = jnp.concatenate([keep(rows), last(rows)], axis=1)
        partner = swapped(jnp.concatenate([give(rows), last(rows)], axis=1), "tm")
        near_own, far_own = to_near(own, "tm"), to_far(own, "tm")
        partner, _ = lax.optimization_barrier((partner, ahead))
        near_partner, far_partner = to_near(partner, "tm"), to_far(partner, "tm")
        return (own, partner, near_own, near_partner, far_own, far_partner)

    value_windows = spread(values)
    query_float = query_raw.astype(jnp.float32)
    key_float = key_raw.astype(jnp.float32)
    shares = jnp.stack(
        [jnp.sum(key_float * key_float, axis=1), jnp.sum(query_float * query_float, axis=1)]
    )
    squares = lax.psum(shares, "head")
    inverses = lax.rsqrt(squares / all_features + NORM_EPSILON)
    key_inverse = inverses[0][:, None]
    query_inverse = inverses[1][:, None]
    query_unit = query_float * query_inverse
    key_unit = key_float * key_inverse
    key_normed = (key_unit * key_gain[None, :]).astype(jnp.bfloat16)
    key_windows = spread(key_normed, value_windows[2:5:2])
    windows = lax.optimization_barrier(key_windows + value_windows)

    query_scaled = (query_unit * (query_gain * (SCALE * LOG2E))[None, :]).astype(jnp.bfloat16)
    given_query, _ = lax.optimization_barrier(
        (jnp.stack([give(query_scaled), give(out_grad)]), key_windows[1])
    )
    given = swapped(given_query, "tm")
    query_pair = jnp.stack([keep(query_scaled), given[0]])
    grad_pair = jnp.stack([keep(out_grad), given[1]])
    query_last = last(query_scaled)[None]
    grad_last = last(out_grad)[None]
    ints, bias = live_tables(chain_pos, groups, block_mask, band_strides)

    def received(result):
        return (to_near(result[2], "tm"), to_far(result[3], "tm"))

    result_last = attention_slot(2, 0, 1, ints, bias, query_last, grad_last, windows)
    received_last = received(result_last)
    result_first = attention_slot(0, 0, 2, ints, bias, query_pair, grad_pair, windows)
    received_first = received(result_first)
    query_gated, rows_to_give, received_last = lax.optimization_barrier(
        (query_pair, result_first[1], received_last)
    )
    rows_first = swapped(rows_to_give, "tm")
    result_second = attention_slot(1, 1, 2, ints, bias, query_gated, grad_pair, windows)
    received_second = received(result_second)
    gains = (result_first[5], result_second[5], result_last[5])

    def placed(mine, theirs, rest):
        first = jnp.where(even, mine, theirs)
        second = jnp.where(even, theirs, mine)
        return jnp.concatenate([first, second, rest], axis=-1)

    taken = jnp.concatenate([gains[0], gains[1]], axis=1)
    gains = placed(taken, jnp.zeros_like(taken), gains[2])
    gains = gains * jnp.stack([1.0 / (query_gain * (SCALE * LOG2E)), LN2 / key_gain])
    gains = summed_over_digit(gains, 1, 2)

    def part_sum(result, pair, start):
        stop = start + 2
        return (
            result[4][start:stop]
            + pair[0][start:stop].astype(jnp.float32)
            + pair[1][start:stop].astype(jnp.float32)
        )

    results = (result_first, result_second, result_last)
    give_first, give_last = (
        part_sum(result, pair, 0).astype(jnp.bfloat16)
        for result, pair in ((result_first, received_first), (result_last, received_last))
    )
    gains, rows_to_give, give_first, give_last = lax.optimization_barrier(
        (gains, result_second[1], give_first, give_last)
    )
    rows_second = swapped(rows_to_give, "tm")
    gains, rows_second = lax.optimization_barrier((gains, rows_second))
    gains = summed_over_digit(gains, 2, 4)
    give_second = part_sum(result_second, received_second, 0).astype(jnp.bfloat16)
    pairs = (received_first, received_second, received_last)
    kept_grads = [part_sum(result, pair, 2) for result, pair in zip(results, pairs)]
    given_grads = [
        swapped(part, "tm").astype(jnp.float32) for part in (give_first, give_second, give_last)
    ]
    gains, given_grads = lax.optimization_barrier((gains, given_grads))
    gains = summed_over_digit(gains, 8, 4)

    rows = placed(
        jnp.concatenate([result_first[0], result_second[0]], axis=2),
        jnp.concatenate([rows_first, rows_second], axis=2),
        result_last[0],
    )
    attended = rows[0]
    grad_query = rows[1].astype(jnp.float32)
    grads = placed(
        jnp.concatenate([kept_grads[0], kept_grads[1]], axis=2),
        jnp.concatenate([given_grads[0], given_grads[1]], axis=2),
        kept_grads[2] + given_grads[2],
    )
    grad_key = grads[0]
    grad_value = grads[1].astype(jnp.bfloat16)
    query_back = grad_query * query_gain[None, :]
    key_back = grad_key * key_gain[None, :]
    inner = lax.psum(
        jnp.stack([jnp.sum(query_back * query_unit, axis=1), jnp.sum(key_back * key_unit, axis=1)]),
        "head",
    )
    inner = inner / all_features
    query_grad = (query_inverse * (query_back - query_unit * inner[0][:, None])).astype(jnp.bfloat16)
    key_grad = (key_inverse * (key_back - key_unit * inner[1][:, None])).astype(jnp.bfloat16)
    return (attended, query_grad, key_grad, grad_value, gains[0], gains[1])


def solution(mesh):
    placed = (
        P("tm", "head"),
        P("tm", "head"),
        P("tm", "head"),
        P("head"),
        P("head"),
        P("tm", "head"),
        P(),
        P(),
    )
    return jax.shard_map(
        shards,
        mesh=mesh,
        in_specs=placed,
        out_specs=(
            P("tm", "head"),
            P("tm", "head"),
            P("tm", "head"),
            P("tm", "head"),
            P("head"),
            P("head"),
        ),
        check_vma=False,
    )
```
